512 devices in a mesh: dp: 32 (over z, x), mp: 16 (over y, core).
Axes of the slice: x: 4, y: 8, z: 8, core: 2. Of those that a mesh axis runs over, the one named last changes fastest.
Arguments:
- activations: bfloat16 [49152, 8192], P('dp', 'mp'), may hold values from -6 to 6
- cotangent: bfloat16 [49152, 1024], P('dp', 'mp'), may hold values from -6 to 6
- key_weight: bfloat16 [8192, 1024], P('mp'), may hold values from -0.1875 to 0.1875
- adapter_down: bfloat16 [32, 64, 8192], P('dp', None, 'mp'), may hold values from -0.0625 to 0.0625
- adapter_up: bfloat16 [32, 64, 1024], P('dp', None, 'mp'), may hold values from -0.1875 to 0.1875
- sequence_tenant: int32 [128], P('dp'), may hold values from 0 to 31
- slot_holder_tenant: int32 [32], replicated, may hold values from 0 to 31, each once
Outputs:
- input_gradient: bfloat16 [49152, 8192], P('dp', 'mp')
- grad_a: float32 [32, 64, 8192], P('dp', None, 'mp')
- grad_b: float32 [32, 64, 1024], P('dp', None, 'mp')
The draws below stay inside these ranges and needn't reach their ends.
All inputs are finite; a program needn't handle non-finite values.
Results may differ from the reference program's by a relative error of at most 0.015.
Values may be sent and summed in bfloat16 or wider, within the bound.
No kernel may reach another device: no remote copies, remote signals or barrier semaphores. Data moves between devices by JAX's collectives and lax.ppermute only.
A program may use at most 64 MiB of HBM per device.

```python
import math
import jax
import jax.numpy as jnp
import numpy as np
from jax import lax

MODEL_WIDTH = 8192
KEY_WIDTH = 1024
ADAPTER_RANK = 64
S_DEV = 4
SEQ_ROWS = 384
TENANT_COUNT = 32
NSEQ = 128
TOKENS = 49152
N_DP = 32


def with_ends(values, stream_key, least, high):
    longest = values.shape.index(max(values.shape))
    spots = []
    for shift in (0, 1):
        where = [jax.random.randint(jax.random.fold_in(stream_key, axis), (), 0, length) for axis, length in enumerate(values.shape)]
        where[longest] = (where[longest] + shift) % values.shape[longest]
        spots.append(tuple(where))
    return values.at[spots[0]].set(least).at[spots[1]].set(high)


def block_scale(key, dims, cuts, low, high):
    gain = 1.0
    for dim, parts in cuts:
        steps = jax.random.uniform(jax.random.fold_in(jax.random.fold_in(key, 6), dim), (parts,), jnp.float32, low / len(cuts), high / len(cuts))
        gain = gain * jnp.repeat(jnp.exp(steps), dims[dim] // parts).reshape((-1,) + (1,) * (len(dims) - 1 - dim))
    return gain


def rank_bounds(count, lean):
    loads = [(1 << 20) // math.isqrt(rank ** lean) + 1 for rank in range(1, count + 1)]
    scale = 1 + sum(loads) // (1 << 30)
    return np.cumsum(np.array([max(1, weight // scale) for weight in loads]))


def ranked(stream_key, shape, amount, lean):
    grid = rank_bounds(amount, lean)
    pick = jax.random.randint(jax.random.fold_in(stream_key, 1), shape, 0, int(grid[amount - 1]))
    standing = jnp.searchsorted(jnp.asarray(grid, jnp.int32), pick, side="right")
    return jax.random.permutation(jax.random.fold_in(stream_key, 2), amount)[standing].astype(jnp.int32)


def centred(key, shape, deviation, bound, shards=(), kind=jnp.bfloat16):
    entries = deviation * jax.random.normal(key, shape, jnp.float32)
    if shards:
        entries = entries * block_scale(key, shape, shards, -0.22, 0.18)
    return jnp.clip(entries, -bound, bound).astype(kind)


def setup_inputs(seed: int = 0) -> dict:
    arg_keys = jax.random.split(jax.random.key(seed), 8)
    activations = centred(arg_keys[0], (TOKENS, MODEL_WIDTH), 1.0, 6.0, ((0, 32), (1, 16)))
    cotangent = centred(arg_keys[1], (TOKENS, KEY_WIDTH), 1.0, 6.0, ((0, 32), (1, 16)))
    key_weight = centred(arg_keys[2], (MODEL_WIDTH, KEY_WIDTH), KEY_WIDTH ** -0.5, 0.1875, ((0, 16),))
    adapter_down = centred(arg_keys[3], (TENANT_COUNT, ADAPTER_RANK, MODEL_WIDTH), MODEL_WIDTH ** -0.5, 0.0625, ((0, 32), (2, 16)))
    adapter_up = centred(arg_keys[4], (TENANT_COUNT, ADAPTER_RANK, KEY_WIDTH), KEY_WIDTH ** -0.5, 0.1875, ((0, 32), (2, 16)))
    sequence_tenant = with_ends(ranked(arg_keys[5], (NSEQ,), TENANT_COUNT, 2), jax.random.fold_in(arg_keys[5], 3), 0, TENANT_COUNT - 1).astype(jnp.int32)
    slot_holder_tenant = jax.random.permutation(arg_keys[6], TENANT_COUNT).astype(jnp.int32)
    return {"activations": activations, "cotangent": cotangent, "key_weight": key_weight, "adapter_down": adapter_down, "adapter_up": adapter_up, "sequence_tenant": sequence_tenant, "slot_holder_tenant": slot_holder_tenant}


ADAPTER_SCALE = 2.0

def reference(activations, cotangent, key_weight, adapter_down, adapter_up, sequence_tenant, slot_holder_tenant):
    scaled_gradient = ADAPTER_SCALE / math.sqrt(S_DEV * SEQ_ROWS)
    slot_of = jnp.argsort(slot_holder_tenant).astype(jnp.int32)
    slots = slot_of[sequence_tenant].astype(jnp.int32)
    x_all = activations.reshape(NSEQ, SEQ_ROWS, MODEL_WIDTH)
    dy_all = cotangent.reshape(NSEQ, SEQ_ROWS, KEY_WIDTH)

    def per_seq(index):
        slot_number = slots[index]
        xq = x_all[index]
        dyq = dy_all[index]
        down_panel_rows = adapter_down[slot_number]
        up_panel_rows = adapter_up[slot_number]
        low_u = jnp.dot(xq, down_panel_rows.T, preferred_element_type=jnp.float32).astype(jnp.bfloat16)
        rank_gradient = jnp.dot(dyq, up_panel_rows.T, preferred_element_type=jnp.float32).astype(jnp.bfloat16)
        activation_gradient = jnp.dot(dyq, key_weight.T, preferred_element_type=jnp.float32)
        activation_gradient = activation_gradient + ADAPTER_SCALE * jnp.dot(rank_gradient, down_panel_rows, preferred_element_type=jnp.float32)
        part_a = scaled_gradient * jnp.dot(rank_gradient.T, xq, preferred_element_type=jnp.float32)
        part_b = scaled_gradient * jnp.dot(low_u.T, dyq, preferred_element_type=jnp.float32)
        return (activation_gradient.astype(jnp.bfloat16), part_a, part_b)
    activation_gradient, part_a, part_b = lax.map(per_seq, jnp.arange(NSEQ, dtype=jnp.int32))
    part_a = part_a.reshape(N_DP, S_DEV, ADAPTER_RANK, MODEL_WIDTH)
    part_b = part_b.reshape(N_DP, S_DEV, ADAPTER_RANK, KEY_WIDTH)
    hits = (sequence_tenant[:, None] == slot_holder_tenant[None, :]).astype(jnp.float32).reshape(N_DP, S_DEV, TENANT_COUNT)

    def add_group(carry, items):
        hit, piece_a, piece_b = items
        term_a = jnp.einsum('st,srd->trd', hit, piece_a, precision=lax.Precision.HIGHEST)
        term_b = jnp.einsum('st,srd->trd', hit, piece_b, precision=lax.Precision.HIGHEST)
        term_a = lax.optimization_barrier(term_a.astype(jnp.bfloat16)).astype(jnp.float32)
        term_b = lax.optimization_barrier(term_b.astype(jnp.bfloat16)).astype(jnp.float32)
        return ((carry[0] + term_a, carry[1] + term_b), None)
    start = (jnp.zeros((TENANT_COUNT, ADAPTER_RANK, MODEL_WIDTH), jnp.float32), jnp.zeros((TENANT_COUNT, ADAPTER_RANK, KEY_WIDTH), jnp.float32))
    (grad_a, grad_b), unused = lax.scan(add_group, start, (hits, part_a, part_b))
    return (activation_gradient.reshape(TOKENS, MODEL_WIDTH), grad_a, grad_b)
```

```python
import math

import jax
import jax.numpy as jnp
from jax import lax
from jax.sharding import PartitionSpec as P

ADAPTER_SCALE = 2.0
F32 = jnp.float32
BF16 = jnp.bfloat16


def local(
    activations,
    cotangent,
    key_weight,
    adapter_down,
    adapter_up,
    sequence_tenant,
    slot_holder_tenant,
):
    seqs = sequence_tenant.shape[0]
    rows = activations.shape[0] // seqs
    width = activations.shape[1]
    keys = cotangent.shape[1]
    rank = adapter_down.shape[1]
    slots = slot_holder_tenant.shape[0]
    scale = ADAPTER_SCALE / math.sqrt(seqs * rows)
    packs = width // keys
    prows = rank // packs

    dy_t = lax.all_gather(cotangent.T, "mp", axis=0, tiled=True)
    groups = dy_t.shape[0] // keys

    up = adapter_up[0].reshape(packs, prows, keys).transpose(1, 0, 2).reshape(prows, width)
    panel = jnp.concatenate([adapter_down[0], up], axis=0)
    sent = jnp.broadcast_to(panel[None], (slots,) + panel.shape)
    panels = lax.all_to_all(sent, "dp", 0, 0, tiled=True)
    hits = sequence_tenant[:, None] == slot_holder_tenant[None, :]
    slot_of = jnp.sum(jnp.where(hits, jnp.arange(slots, dtype=jnp.int32)[None, :], 0), axis=1)
    picked = jnp.stack(
        [lax.dynamic_index_in_dim(panels, slot_of[s], 0, keepdims=False) for s in range(seqs)]
    )
    pick_a = picked[:, :rank]
    pick_b = (
        picked[:, rank:].reshape(seqs, prows, packs, keys).transpose(0, 2, 1, 3).reshape(seqs, rank, keys)
    )

    x_seq = activations.reshape(seqs, rows, width)
    dy_seq = dy_t.reshape(groups * keys, seqs, rows)
    low_u = jnp.einsum("snd,srd->snr", x_seq, pick_a, preferred_element_type=F32).astype(BF16)
    part_b = jnp.einsum("ksn,snr->skr", dy_seq, low_u, preferred_element_type=F32).astype(BF16)
    part_b = part_b.reshape(seqs, groups, keys, rank).transpose(1, 0, 2, 3)
    spread_b = jnp.broadcast_to(pick_b.transpose(0, 2, 1)[None], (groups, seqs, keys, rank))
    got = lax.all_to_all(jnp.concatenate([part_b, spread_b], axis=3), "mp", 0, 0, tiled=True)
    seq_b = scale * jnp.sum(got[..., :rank].astype(F32), axis=0)
    full_b = got[..., rank:].transpose(1, 0, 2, 3).reshape(seqs, groups * keys, rank)

    low_g = jnp.einsum("ksn,skr->srn", dy_seq, full_b, preferred_element_type=F32).astype(BF16)
    seq_a = scale * jnp.einsum("srn,snd->srd", low_g, x_seq, preferred_element_type=F32)

    owner_a = [jnp.sum(jnp.where(hits[:, t, None, None], seq_a, 0.0), axis=0) for t in range(slots)]
    owner_a = jnp.stack(owner_a).astype(BF16)
    owner_b = [jnp.sum(jnp.where(hits[:, t, None, None], seq_b, 0.0), axis=0) for t in range(slots)]
    owner_b = jnp.stack(owner_b).astype(BF16).transpose(0, 2, 1)
    owner_b = owner_b.reshape(slots, packs, prows, keys).transpose(0, 2, 1, 3).reshape(slots, prows, width)
    parts = lax.all_to_all(jnp.concatenate([owner_a, owner_b], axis=1), "dp", 0, 0, tiled=True)
    total = jnp.sum(parts.astype(F32), axis=0)
    grad_a = total[None, :rank]
    grad_b = total[rank:].reshape(prows, packs, keys).transpose(1, 0, 2).reshape(1, rank, keys)

    frozen = lax.dot_general(
        dy_t, key_weight, (((0,), (1,)), ((), ())), preferred_element_type=F32
    )
    update = jnp.einsum("srn,srd->snd", low_g, pick_a, preferred_element_type=F32)
    input_gradient = (frozen + ADAPTER_SCALE * update.reshape(-1, width)).astype(BF16)
    return (input_gradient, grad_a, grad_b)


def solution(mesh):
    in_specs = (
        P("dp", "mp"),
        P("dp", "mp"),
        P("mp", None),
        P("dp", None, "mp"),
        P("dp", None, "mp"),
        P("dp"),
        P(),
    )
    out_specs = (P("dp", "mp"), P("dp", None, "mp"), P("dp", None, "mp"))
    return jax.shard_map(local, mesh=mesh, in_specs=in_specs, out_specs=out_specs, check_vma=False)
```

```python
import functools
import math

import jax
import jax.numpy as jnp
from jax import lax
from jax.experimental import pallas as pl
from jax.experimental.pallas import tpu as pltpu
from jax.sharding import Mesh, PartitionSpec as P

ADAPTER_SCALE = 2.0
F32 = jnp.float32
BF16 = jnp.bfloat16
LANES = 128
COLUMNS = 4
PARAMS = pltpu.CompilerParams(vmem_limit_bytes=40 * 2**20)
SERIAL = pltpu.CompilerParams(
    vmem_limit_bytes=40 * 2**20, dimension_semantics=("arbitrary",)
)
VMEM = pl.BlockSpec(memory_space=pltpu.VMEM)
SMEM = pl.BlockSpec(memory_space=pltpu.SMEM)


def left_half(shape):
    return lax.broadcasted_iota(jnp.int32, shape, 1) < LANES // 2


def pack(tall):
    slabs = []
    for i in range(0, tall.shape[0], 16):
        upper, lower = tall[i : i + 8], pltpu.roll(tall[i + 8 : i + 16], LANES // 2, 1)
        slabs.append(jnp.where(left_half(upper.shape), upper, lower))
    return jnp.concatenate(slabs, axis=1)


def unpack(flat, right):
    pieces = []
    for i in range(0, flat.shape[1], LANES):
        slab = flat[:, i : i + LANES]
        turned = pltpu.roll(slab, LANES // 2, 1)
        left = left_half(slab.shape)
        for piece in (turned, slab) if right else (slab, turned):
            pieces.append(jnp.where(left != right, piece, 0.0))
    return jnp.concatenate(pieces, axis=0)


def prepare(tenant_ref, holder_ref, down_ref, up_ref, sent_ref, slot_ref):
    for s in range(tenant_ref.shape[0]):
        slot = jnp.int32(0)
        for t in range(holder_ref.shape[0]):
            slot = jnp.where(holder_ref[t] == tenant_ref[s], jnp.int32(t), slot)
        slot_ref[s] = slot
    up = up_ref[0].astype(F32).T
    packed = pack(jnp.concatenate([up, jnp.zeros_like(up)], axis=1))
    panel = jnp.concatenate([down_ref[0].astype(F32), packed], axis=0).astype(BF16)
    for z in range(sent_ref.shape[0]):
        sent_ref[z] = panel


def project(slot_ref, panel_ref, x_ref, dy_ref, sent_ref, down_ref):
    rank = down_ref.shape[1]
    groups, _, keys, _ = sent_ref.shape
    panel = panel_ref[0, 0]
    down = panel[:rank]
    wide = jnp.concatenate([down, jnp.zeros_like(down)], axis=0)
    low_u = lax.dot_general(
        x_ref[...], wide, (((1,), (1,)), ((), ())), preferred_element_type=F32
    ).astype(BF16)
    part = jnp.dot(dy_ref[...], low_u, preferred_element_type=F32)
    up = unpack(panel.astype(F32)[rank:], True)
    sent_ref[:, 0] = (part.reshape(groups, keys, 2 * rank) + up[None]).astype(BF16)
    down_ref[0] = down


def combine(
    scale,
    slot_ref,
    got_ref,
    dy_ref,
    x_ref,
    weight_ref,
    down_ref,
    input_ref,
    sent_ref,
):
    rank, width = down_ref.shape[1:]
    columns = sent_ref.shape[0]
    got = got_ref[:, 0]
    dy = dy_ref[...]
    both = lax.dot_general(
        got.reshape(-1, 2 * rank), dy, (((0,), (0,)), ((), ())), preferred_element_type=F32
    )
    low_g = both[rank:].astype(BF16)
    part_a = jnp.dot(low_g, x_ref[...], preferred_element_type=F32)
    part_b = jnp.sum(got.astype(F32), axis=0)
    slot = slot_ref[pl.program_id(0)]
    for x in range(columns):
        place = jnp.where(slot % columns == x, slot // columns, -1).astype(F32)
        tail = jnp.concatenate([scale * pack(part_b), jnp.full((8, width), place, F32)], axis=0)
        sent_ref[x, 0] = jnp.concatenate([scale * part_a, tail], axis=0).astype(BF16)
    frozen = lax.dot_general(
        dy, weight_ref[...], (((0,), (1,)), ((), ())), preferred_element_type=F32
    )
    update = lax.dot_general(
        low_g, down_ref[0], (((0,), (0,)), ((), ())), preferred_element_type=F32
    )
    input_ref[...] = (frozen + ADAPTER_SCALE * update).astype(BF16)


def sort(got_ref, sent_ref):
    columns, seqs = got_ref.shape[:2]
    tall = sent_ref.shape[1]
    rank = tall - 8
    for z in range(sent_ref.shape[0]):
        head = tail = 0.0
        for x in range(columns):
            for s in range(seqs):
                low = got_ref[x, s, rank:].astype(F32)
                here = low[8:9] == z
                head = head + jnp.where(here, got_ref[x, s, :rank].astype(F32), 0.0)
                tail = tail + jnp.where(here, low[:8], 0.0)
        sent_ref[z] = jnp.concatenate([head, tail], axis=0).astype(BF16)


def finish(got_ref, down_ref, up_ref):
    rank = down_ref.shape[1]
    total = got_ref[0].astype(F32)
    for p in range(1, got_ref.shape[0]):
        total = total + got_ref[p].astype(F32)
    down_ref[0] = total[:rank]
    up_ref[0] = unpack(total[rank:], False)[:, :rank].T


def local(
    columns,
    activations,
    cotangent,
    key_weight,
    adapter_down,
    adapter_up,
    sequence_tenant,
    slot_holder_tenant,
):
    seqs = sequence_tenant.shape[0]
    rows = activations.shape[0] // seqs
    width = activations.shape[1]
    keys = cotangent.shape[1]
    rank = adapter_down.shape[1]
    slots = slot_holder_tenant.shape[0]
    tall = rank + rank * keys // width
    scale = ADAPTER_SCALE / math.sqrt(seqs * rows)
    struct = jax.ShapeDtypeStruct

    dy = lax.all_gather(cotangent.T, "mp", axis=0, tiled=True)
    key_width = dy.shape[0]
    groups = key_width // keys

    sent, slot_of = pl.pallas_call(
        prepare,
        out_shape=(struct((slots // columns, tall, width), BF16), struct((seqs,), jnp.int32)),
        in_specs=[SMEM, SMEM, VMEM, VMEM],
        out_specs=(VMEM, SMEM),
        compiler_params=PARAMS,
        name="prepare",
    )(sequence_tenant, slot_holder_tenant, adapter_down, adapter_up)
    panels = lax.all_to_all(sent, "z", 0, 0, tiled=True)
    panels = jnp.broadcast_to(panels[None], (columns,) + panels.shape)
    panels = lax.all_to_all(panels, "x", 0, 0, tiled=True)

    sent, down = pl.pallas_call(
        project,
        grid_spec=pltpu.PrefetchScalarGridSpec(
            num_scalar_prefetch=1,
            grid=(seqs,),
            in_specs=[
                pl.BlockSpec(
                    (1, 1, tall, width),
                    lambda s, slot: (slot[s] % columns, slot[s] // columns, 0, 0),
                ),
                pl.BlockSpec((rows, width), lambda s, slot: (s, 0)),
                pl.BlockSpec((key_width, rows), lambda s, slot: (0, s)),
            ],
            out_specs=(
                pl.BlockSpec((groups, 1, keys, 2 * rank), lambda s, slot: (0, s, 0, 0)),
                pl.BlockSpec((1, rank, width), lambda s, slot: (s, 0, 0)),
            ),
        ),
        out_shape=(
            struct((groups, seqs, keys, 2 * rank), BF16),
            struct((seqs, rank, width), BF16),
        ),
        compiler_params=SERIAL,
        name="project",
    )(slot_of, panels, activations, dy)
    got = lax.all_to_all(sent, "mp", 0, 0, tiled=True)

    input_gradient, sent = pl.pallas_call(
        functools.partial(combine, scale),
        grid_spec=pltpu.PrefetchScalarGridSpec(
            num_scalar_prefetch=1,
            grid=(seqs,),
            in_specs=[
                pl.BlockSpec((groups, 1, keys, 2 * rank), lambda s, slot: (0, s, 0, 0)),
                pl.BlockSpec((key_width, rows), lambda s, slot: (0, s)),
                pl.BlockSpec((rows, width), lambda s, slot: (s, 0)),
                pl.BlockSpec((width, key_width), lambda s, slot: (0, 0)),
                pl.BlockSpec((1, rank, width), lambda s, slot: (s, 0, 0)),
            ],
            out_specs=(
                pl.BlockSpec((rows, width), lambda s, slot: (s, 0)),
                pl.BlockSpec((columns, 1, tall + 8, width), lambda s, slot: (0, s, 0, 0)),
            ),
        ),
        out_shape=(
            struct(activations.shape, BF16),
            struct((columns, seqs, tall + 8, width), BF16),
        ),
        compiler_params=SERIAL,
        name="combine",
    )(slot_of, got, dy, activations, key_weight, down)
    got = lax.all_to_all(sent, "x", 0, 0, tiled=True)

    sent = pl.pallas_call(
        sort,
        out_shape=struct((slots // columns, tall, width), BF16),
        in_specs=[VMEM],
        out_specs=VMEM,
        compiler_params=PARAMS,
        name="sort",
    )(got)
    got = lax.all_to_all(sent, "z", 0, 0, tiled=True)

    grad_a, grad_b = pl.pallas_call(
        finish,
        out_shape=(struct((1, rank, width), F32), struct((1, rank, keys), F32)),
        in_specs=[VMEM],
        out_specs=(VMEM, VMEM),
        compiler_params=PARAMS,
        name="finish",
    )(got)
    return (input_gradient, grad_a, grad_b)


def solution(mesh):
    columns = min(COLUMNS, mesh.shape["dp"] // 2)
    grid = Mesh(mesh.devices.reshape(-1, columns, mesh.shape["mp"]), ("z", "x", "mp"))
    dp = ("z", "x")
    in_specs = (
        P(dp, "mp"),
        P(dp, "mp"),
        P("mp", None),
        P(dp, None, "mp"),
        P(dp, None, "mp"),
        P(dp),
        P(),
    )
    out_specs = (P(dp, "mp"), P(dp, None, "mp"), P(dp, None, "mp"))
    body = functools.partial(local, columns)
    return jax.shard_map(body, mesh=grid, in_specs=in_specs, out_specs=out_specs, check_vma=False)
```

```python
import functools
import math

import jax
import jax.numpy as jnp
from jax import lax
from jax.experimental import pallas as pl
from jax.experimental.pallas import tpu as pltpu
from jax.sharding import Mesh, PartitionSpec as P

ADAPTER_SCALE = 2.0
F32 = jnp.float32
BF16 = jnp.bfloat16
LANES = 128
COLUMNS = 4
ALL = pltpu.CompilerParams(vmem_limit_bytes=58 * 2**20, dimension_semantics=("arbitrary",))
WHOLE = pltpu.CompilerParams(vmem_limit_bytes=58 * 2**20)
PART = pltpu.CompilerParams(vmem_limit_bytes=24 * 2**20)
VMEM = pl.BlockSpec(memory_space=pltpu.VMEM)
SMEM = pl.BlockSpec(memory_space=pltpu.SMEM)


def left_half(shape):
    return lax.broadcasted_iota(jnp.int32, shape, 1) < LANES // 2


def pack(tall):
    slabs = []
    for i in range(0, tall.shape[0], 16):
        upper, lower = tall[i : i + 8], pltpu.roll(tall[i + 8 : i + 16], LANES // 2, 1)
        slabs.append(jnp.where(left_half(upper.shape), upper, lower))
    return jnp.concatenate(slabs, axis=1)


def unpack(flat, right):
    pieces = []
    for i in range(0, flat.shape[1], LANES):
        slab = flat[:, i : i + LANES]
        turned = pltpu.roll(slab, LANES // 2, 1)
        left = left_half(slab.shape)
        for piece in (turned, slab) if right else (slab, turned):
            pieces.append(jnp.where(left != right, piece, 0.0))
    return jnp.concatenate(pieces, axis=0)


def prepare(down_ref, up_ref, sent_ref):
    up = up_ref[0].astype(F32).T
    packed = pack(jnp.concatenate([up, jnp.zeros_like(up)], axis=1))
    panel = jnp.concatenate([down_ref[0].astype(F32), packed], axis=0).astype(BF16)
    for z in range(sent_ref.shape[0]):
        sent_ref[z] = panel


def select(columns, panel_ref, holder_ref, *refs):
    tenant_refs, (sent_ref, slot_ref, table) = refs[:columns], refs[columns:]
    for t in range(holder_ref.shape[0]):
        table[holder_ref[t]] = jnp.int32(t)
    here = lax.axis_index("x")
    for back, tenant_ref in enumerate(tenant_refs):
        there = lax.rem(here + columns - back, columns)
        for s in range(tenant_ref.shape[0]):
            slot = table[tenant_ref[s]]
            if back == 0:
                slot_ref[s] = slot
            sent_ref[there, s] = panel_ref[slot // columns]


def project(slot_ref, panel_ref, x_ref, dy_ref, sent_ref, down_ref):
    rank = down_ref.shape[1]
    groups, _, keys, _ = sent_ref.shape
    panel = panel_ref[0, 0]
    down = panel[:rank]
    wide = jnp.concatenate([down, jnp.zeros_like(down)], axis=0)
    low_u = lax.dot_general(
        x_ref[...], wide, (((1,), (1,)), ((), ())), preferred_element_type=F32
    ).astype(BF16)
    part = jnp.dot(dy_ref[...], low_u, preferred_element_type=F32)
    up = unpack(panel.astype(F32)[rank:], True)
    sent_ref[:, 0] = (part.reshape(groups, keys, 2 * rank) + up[None]).astype(BF16)
    down_ref[0] = down


def combine(
    scale,
    slot_ref,
    got_ref,
    dy_ref,
    x_ref,
    low_ref,
    sent_ref,
):
    rank, width = low_ref.shape[1], x_ref.shape[1]
    columns = sent_ref.shape[0]
    got = got_ref[:, 0]
    dy = dy_ref[...]
    both = lax.dot_general(
        got.reshape(-1, 2 * rank), dy, (((0,), (0,)), ((), ())), preferred_element_type=F32
    )
    low_g = both[rank:].astype(BF16)
    low_ref[0] = low_g
    part_a = jnp.dot(low_g, x_ref[...], preferred_element_type=F32)
    part_b = jnp.sum(got.astype(F32), axis=0)
    slot = slot_ref[pl.program_id(0)]
    for x in range(columns):
        place = jnp.where(slot % columns == x, slot // columns, -1).astype(F32)
        tail = jnp.concatenate([scale * pack(part_b), jnp.full((8, width), place, F32)], axis=0)
        sent_ref[x, 0] = jnp.concatenate([scale * part_a, tail], axis=0).astype(BF16)


def backward(low_ref, dy_ref, weight_ref, down_ref, input_ref):
    frozen = lax.dot_general(
        dy_ref[...], weight_ref[...], (((0,), (1,)), ((), ())), preferred_element_type=F32
    )
    update = lax.dot_general(
        low_ref[0], down_ref[0], (((0,), (0,)), ((), ())), preferred_element_type=F32
    )
    input_ref[...] = (frozen + ADAPTER_SCALE * update).astype(BF16)


def sort(got_ref, sent_ref):
    columns, seqs = got_ref.shape[:2]
    tall = sent_ref.shape[1]
    rank = tall - 8
    for z in range(sent_ref.shape[0]):
        head = tail = 0.0
        for x in range(columns):
            for s in range(seqs):
                low = got_ref[x, s, rank:].astype(F32)
                here = low[8:9] == z
                head = head + jnp.where(here, got_ref[x, s, :rank].astype(F32), 0.0)
                tail = tail + jnp.where(here, low[:8], 0.0)
        sent_ref[z] = jnp.concatenate([head, tail], axis=0).astype(BF16)


def finish(got_ref, down_ref, up_ref):
    rank = down_ref.shape[1]
    total = got_ref[0].astype(F32)
    for p in range(1, got_ref.shape[0]):
        total = total + got_ref[p].astype(F32)
    down_ref[0] = total[:rank]
    up_ref[0] = unpack(total[rank:], False)[:, :rank].T


def local(
    columns,
    activations,
    cotangent,
    key_weight,
    adapter_down,
    adapter_up,
    sequence_tenant,
    slot_holder_tenant,
):
    seqs = sequence_tenant.shape[0]
    rows = activations.shape[0] // seqs
    width = activations.shape[1]
    keys = cotangent.shape[1]
    rank = adapter_down.shape[1]
    slots = slot_holder_tenant.shape[0]
    tall = rank + rank * keys // width
    scale = ADAPTER_SCALE / math.sqrt(seqs * rows)
    struct = jax.ShapeDtypeStruct

    dy = lax.all_gather(cotangent.T, "mp", axis=0, tiled=True)
    key_width = dy.shape[0]
    groups = key_width // keys

    tenants = [sequence_tenant] + [
        lax.ppermute(sequence_tenant, "x", [(x, (x + d) % columns) for x in range(columns)])
        for d in range(1, columns)
    ]
    sent = pl.pallas_call(
        prepare,
        out_shape=struct((slots // columns, tall, width), BF16),
        in_specs=[VMEM, VMEM],
        out_specs=VMEM,
        compiler_params=WHOLE,
        name="prepare",
    )(adapter_down, adapter_up)
    panels = lax.all_to_all(sent, "z", 0, 0, tiled=True)
    sent, slot_of = pl.pallas_call(
        functools.partial(select, columns),
        out_shape=(
            struct((columns, seqs, tall, width), BF16),
            struct((seqs,), jnp.int32),
        ),
        in_specs=[VMEM] + [SMEM] * (1 + columns),
        out_specs=(VMEM, SMEM),
        scratch_shapes=[pltpu.SMEM((slots,), jnp.int32)],
        compiler_params=PART,
        name="select",
    )(panels, slot_holder_tenant, *tenants)
    panels = lax.all_to_all(sent, "x", 0, 0, tiled=True)

    sent, down = pl.pallas_call(
        project,
        grid_spec=pltpu.PrefetchScalarGridSpec(
            num_scalar_prefetch=1,
            grid=(seqs,),
            in_specs=[
                pl.BlockSpec(
                    (1, 1, tall, width),
                    lambda s, slot: (slot[s] % columns, s, 0, 0),
                ),
                pl.BlockSpec((rows, width), lambda s, slot: (s, 0)),
                pl.BlockSpec((key_width, rows), lambda s, slot: (0, s)),
            ],
            out_specs=(
                pl.BlockSpec((groups, 1, keys, 2 * rank), lambda s, slot: (0, s, 0, 0)),
                pl.BlockSpec((1, rank, width), lambda s, slot: (s, 0, 0)),
            ),
        ),
        out_shape=(
            struct((groups, seqs, keys, 2 * rank), BF16),
            struct((seqs, rank, width), BF16),
        ),
        compiler_params=ALL,
        name="project",
    )(slot_of, panels, activations, dy)
    got = lax.all_to_all(sent, "mp", 0, 0, tiled=True)

    low_g, sent = pl.pallas_call(
        functools.partial(combine, scale),
        grid_spec=pltpu.PrefetchScalarGridSpec(
            num_scalar_prefetch=1,
            grid=(seqs,),
            in_specs=[
                pl.BlockSpec((groups, 1, keys, 2 * rank), lambda s, slot: (0, s, 0, 0)),
                pl.BlockSpec((key_width, rows), lambda s, slot: (0, s)),
                pl.BlockSpec((rows, width), lambda s, slot: (s, 0)),
            ],
            out_specs=(
                pl.BlockSpec((1, rank, rows), lambda s, slot: (s, 0, 0)),
                pl.BlockSpec((columns, 1, tall + 8, width), lambda s, slot: (0, s, 0, 0)),
            ),
        ),
        out_shape=(
            struct((seqs, rank, rows), BF16),
            struct((columns, seqs, tall + 8, width), BF16),
        ),
        compiler_params=ALL,
        name="combine",
    )(slot_of, got, dy, activations)
    input_gradient = pl.pallas_call(
        backward,
        grid=(seqs,),
        in_specs=[
            pl.BlockSpec((1, rank, rows), lambda s: (s, 0, 0)),
            pl.BlockSpec((key_width, rows), lambda s: (0, s)),
            pl.BlockSpec((width, key_width), lambda s: (0, 0)),
            pl.BlockSpec((1, rank, width), lambda s: (s, 0, 0)),
        ],
        out_specs=pl.BlockSpec((rows, width), lambda s: (s, 0)),
        out_shape=struct(activations.shape, BF16),
        compiler_params=ALL,
        cost_estimate=pl.CostEstimate(
            flops=2 * activations.shape[0] * width * (key_width + rank),
            bytes_accessed=2 * (activations.shape[0] + width) * (key_width + width),
            transcendentals=0,
        ),
        name="backward",
    )(low_g, dy, key_weight, down)
    got = lax.all_to_all(sent, "x", 0, 0, tiled=True)

    sent = pl.pallas_call(
        sort,
        out_shape=struct((slots // columns, tall, width), BF16),
        in_specs=[VMEM],
        out_specs=VMEM,
        compiler_params=PART,
        name="sort",
    )(got)
    got = lax.all_to_all(sent, "z", 0, 0, tiled=True)

    grad_a, grad_b = pl.pallas_call(
        finish,
        out_shape=(struct((1, rank, width), F32), struct((1, rank, keys), F32)),
        in_specs=[VMEM],
        out_specs=(VMEM, VMEM),
        compiler_params=PART,
        name="finish",
    )(got)
    return (input_gradient, grad_a, grad_b)


def solution(mesh):
    columns = min(COLUMNS, mesh.shape["dp"] // 2)
    grid = Mesh(mesh.devices.reshape(-1, columns, mesh.shape["mp"]), ("z", "x", "mp"))
    dp = ("z", "x")
    in_specs = (
        P(dp, "mp"),
        P(dp, "mp"),
        P("mp", None),
        P(dp, None, "mp"),
        P(dp, None, "mp"),
        P(dp),
        P(),
    )
    out_specs = (P(dp, "mp"), P(dp, None, "mp"), P(dp, None, "mp"))
    body = functools.partial(local, columns)
    return jax.shard_map(body, mesh=grid, in_specs=in_specs, out_specs=out_specs, check_vma=False)
```

```python
import functools
import math

import jax
import jax.numpy as jnp
from jax import lax
from jax.experimental import pallas as pl
from jax.experimental.pallas import tpu as pltpu
from jax.sharding import Mesh, PartitionSpec as P

ADAPTER_SCALE = 2.0
F32 = jnp.float32
BF16 = jnp.bfloat16
LANES = 128
COLUMNS = 4
SWAP = [(0, 1), (1, 0)]
WHOLE = pltpu.CompilerParams(vmem_limit_bytes=58 * 2**20)
ALL = pltpu.CompilerParams(vmem_limit_bytes=58 * 2**20, dimension_semantics=("arbitrary",))
STEPS = pltpu.CompilerParams(vmem_limit_bytes=24 * 2**20, dimension_semantics=("arbitrary",))
PART = pltpu.CompilerParams(vmem_limit_bytes=24 * 2**20)
VMEM = pl.BlockSpec(memory_space=pltpu.VMEM)
SMEM = pl.BlockSpec(memory_space=pltpu.SMEM)


def left_half(shape):
    return lax.broadcasted_iota(jnp.int32, shape, 1) < LANES // 2


def pack(tall):
    slabs = []
    for i in range(0, tall.shape[0], 16):
        upper, lower = tall[i : i + 8], pltpu.roll(tall[i + 8 : i + 16], LANES // 2, 1)
        slabs.append(jnp.where(left_half(upper.shape), upper, lower))
    return jnp.concatenate(slabs, axis=1)


def unpack(flat, right):
    pieces = []
    for i in range(0, flat.shape[1], LANES):
        slab = flat[:, i : i + LANES]
        turned = pltpu.roll(slab, LANES // 2, 1)
        left = left_half(slab.shape)
        for piece in (turned, slab) if right else (slab, turned):
            pieces.append(jnp.where(left != right, piece, 0.0))
    return jnp.concatenate(pieces, axis=0)


def prepare(down_ref, up_ref, sent_ref):
    up = up_ref[0].astype(F32).T
    packed = pack(jnp.concatenate([up, jnp.zeros_like(up)], axis=1))
    panel = jnp.concatenate([down_ref[0].astype(F32), packed], axis=0).astype(BF16)
    for z in range(sent_ref.shape[0]):
        sent_ref[z] = panel


def select(columns, panel_ref, holder_ref, *refs):
    tenant_refs, (sent_ref, slot_ref, table) = refs[:columns], refs[-3:]
    for t in range(holder_ref.shape[0]):
        table[holder_ref[t]] = jnp.int32(t)
    here = lax.axis_index("x")
    for back, tenant_ref in enumerate(tenant_refs):
        there = lax.rem(here + columns - back, columns)
        for s in range(tenant_ref.shape[0]):
            slot = table[tenant_ref[s]]
            if back == 0:
                slot_ref[s] = slot
            sent_ref[there, s] = panel_ref[slot // columns]


def stack(chips, *refs):
    slices, (out_ref, sem) = refs[:chips], refs[chips:]
    here = lax.axis_index("y")
    copies = []
    for back, ref in enumerate(slices):
        there = lax.rem(here + chips - back, chips)
        copies.append(pltpu.make_async_copy(ref, out_ref.at[there], sem.at[back]))
        copies[-1].start()
    for copy in copies:
        copy.wait()


def low(slot_ref, panel0_ref, panel1_ref, x_ref, low_ref, down_ref, ups_ref):
    rank = down_ref.shape[1]
    rows = low_ref.shape[1]
    total = ups = 0.0
    for side, panel_ref in enumerate((panel0_ref, panel1_ref)):
        panel = panel_ref[0, 0]
        down = panel[:rank]
        down_ref[side] = down
        blank = jnp.zeros_like(down)
        wide = jnp.concatenate([blank, down] if side else [down, blank], axis=0)
        total = total + lax.dot_general(
            x_ref[side * rows : (side + 1) * rows],
            wide,
            (((1,), (1,)), ((), ())),
            preferred_element_type=F32,
        )
        ups = ups + unpack(panel.astype(F32)[rank:], side == 1)
    low_ref[0] = total.astype(BF16)
    ups_ref[0] = ups.astype(BF16)


def project(low_ref, other_ref, ups_ref, dy_ref, sent_ref):
    rows = low_ref.shape[1]
    chips, keys, _ = dy_ref.shape
    low_u = (low_ref[0].astype(F32) + other_ref[0].astype(F32)).astype(BF16)
    dy = dy_ref[...].reshape(chips * keys, 2 * rows)
    parts = [
        jnp.dot(dy[:, side * rows : (side + 1) * rows], low_u, preferred_element_type=F32)
        for side in range(2)
    ]
    part = jnp.where(left_half(parts[0].shape), parts[0], parts[1])
    sent_ref[:, 0, :keys] = part.reshape(chips, keys, LANES).astype(BF16)
    for y in range(chips):
        sent_ref[y, 0, keys:] = ups_ref[0]


def lower(got_ref, dy_ref, low_ref):
    _, rank, rows = low_ref.shape
    chips, keys, _ = dy_ref.shape
    ups = got_ref[:, 0, keys:].reshape(chips * keys, LANES)
    dy = dy_ref[...].reshape(chips * keys, 2 * rows)
    for side in range(2):
        both = lax.dot_general(
            ups,
            dy[:, side * rows : (side + 1) * rows],
            (((0,), (0,)), ((), ())),
            preferred_element_type=F32,
        )
        low_ref[side] = both[side * rank : (side + 1) * rank].astype(BF16)


def tally(scale, got_ref, part_ref):
    keys = got_ref.shape[2] // 2
    for pair in range(got_ref.shape[1]):
        total = 0.0
        for y in range(got_ref.shape[0]):
            total = total + got_ref[y, pair, :keys].astype(F32)
        total = scale * total
        part_ref[2 * pair] = pack(total)
        part_ref[2 * pair + 1] = pack(pltpu.roll(total, LANES // 2, 1))


def combine(scale, slot_ref, low_ref, other_ref, part_ref, x_ref, low_g_ref, sent_ref):
    columns = sent_ref.shape[0]
    width = x_ref.shape[1]
    low_g = (low_ref[0].astype(F32) + other_ref[0].astype(F32)).astype(BF16)
    low_g_ref[0] = low_g
    part_a = scale * jnp.dot(low_g, x_ref[...], preferred_element_type=F32)
    part_a = part_a.astype(BF16)
    rank = part_a.shape[0]
    slot = slot_ref[pl.program_id(0)]
    for x in range(columns):
        place = jnp.where(slot % columns == x, slot // columns, -1).astype(F32)
        tail = jnp.concatenate([part_ref[0], jnp.full((8, width), place, F32)], axis=0)
        sent_ref[x, 0, :rank] = part_a
        sent_ref[x, 0, rank:] = tail.astype(BF16)


def backward(low_ref, dy_ref, other_ref, weight_ref, down_ref, input_ref):
    first = lax.axis_index("c") == 0
    dy, other = dy_ref[...], other_ref[...]
    both = jnp.concatenate(
        [jnp.where(first, dy, other), jnp.where(first, other, dy)], axis=1
    )
    frozen = lax.dot_general(
        both.reshape(-1, dy.shape[2]),
        weight_ref[...],
        (((0,), (1,)), ((), ())),
        preferred_element_type=F32,
    )
    update = lax.dot_general(
        low_ref[0], down_ref[0], (((0,), (0,)), ((), ())), preferred_element_type=F32
    )
    input_ref[...] = (frozen + ADAPTER_SCALE * update).astype(BF16)


def sort(got_ref, sent_ref):
    columns, seqs = got_ref.shape[:2]
    tall = sent_ref.shape[1]
    rank = tall - 8
    for z in range(sent_ref.shape[0]):
        head = tail = 0.0
        for x in range(columns):
            for s in range(seqs):
                low = got_ref[x, s, rank:].astype(F32)
                here = low[8:9] == z
                head = head + jnp.where(here, got_ref[x, s, :rank].astype(F32), 0.0)
                tail = tail + jnp.where(here, low[:8], 0.0)
        sent_ref[z] = jnp.concatenate([head, tail], axis=0).astype(BF16)


def finish(got_ref, down_ref, up_ref):
    rank = down_ref.shape[1]
    total = got_ref[0].astype(F32)
    for p in range(1, got_ref.shape[0]):
        total = total + got_ref[p].astype(F32)
    down_ref[0] = total[:rank]
    up_ref[0] = unpack(total[rank:], False)[:, :rank].T


def local(
    columns,
    chips,
    activations,
    cotangent,
    key_weight,
    adapter_down,
    adapter_up,
    sequence_tenant,
    slot_holder_tenant,
):
    seqs = sequence_tenant.shape[0]
    rows = activations.shape[0] // seqs
    width = activations.shape[1]
    keys = cotangent.shape[1]
    rank = adapter_down.shape[1]
    slots = slot_holder_tenant.shape[0]
    tall = rank + rank * keys // width
    scale = ADAPTER_SCALE / math.sqrt(seqs * rows)
    struct = jax.ShapeDtypeStruct

    own = cotangent.T
    slices = [own] + [
        lax.ppermute(own, "y", [(y, (y + d) % chips) for y in range(chips)])
        for d in range(1, chips)
    ]
    near = [slices[d] for d in sorted({1, 2, chips - 2, chips - 1} & set(range(1, chips)))]
    anywhere = pl.BlockSpec(memory_space=pl.ANY)
    dy = pl.pallas_call(
        functools.partial(stack, chips),
        out_shape=struct((chips,) + own.shape, BF16),
        in_specs=[anywhere] * chips,
        out_specs=anywhere,
        scratch_shapes=[pltpu.SemaphoreType.DMA((chips,))],
        compiler_params=PART,
        name="stack",
    )(*slices)
    other_dy = lax.ppermute(dy, "c", SWAP)

    tenants = [sequence_tenant] + [
        lax.ppermute(sequence_tenant, "x", [(x, (x + d) % columns) for x in range(columns)])
        for d in range(1, columns)
    ]
    sent = pl.pallas_call(
        prepare,
        out_shape=struct((slots // columns, tall, width), BF16),
        in_specs=[VMEM, VMEM],
        out_specs=VMEM,
        compiler_params=WHOLE,
        name="prepare",
    )(adapter_down, adapter_up)
    panels = lax.all_to_all(sent, "z", 0, 0, tiled=True)
    sent, slot_of = pl.pallas_call(
        functools.partial(select, columns),
        out_shape=(
            struct((columns, seqs, tall, width), BF16),
            struct((seqs,), jnp.int32),
        ),
        in_specs=[VMEM] + [SMEM] * (1 + columns) + [anywhere] * len(near),
        out_specs=(VMEM, SMEM),
        scratch_shapes=[pltpu.SMEM((slots,), jnp.int32)],
        compiler_params=PART,
        name="select",
    )(panels, slot_holder_tenant, *tenants, *near)
    panels = lax.all_to_all(sent, "x", 0, 0, tiled=True)

    pairs = seqs // 2
    low_u, down, ups = pl.pallas_call(
        low,
        grid_spec=pltpu.PrefetchScalarGridSpec(
            num_scalar_prefetch=1,
            grid=(pairs,),
            in_specs=[
                pl.BlockSpec(
                    (1, 1, tall, width),
                    lambda p, slot: (slot[2 * p] % columns, 2 * p, 0, 0),
                ),
                pl.BlockSpec(
                    (1, 1, tall, width),
                    lambda p, slot: (slot[2 * p + 1] % columns, 2 * p + 1, 0, 0),
                ),
                pl.BlockSpec((2 * rows, width), lambda p, slot: (p, 0)),
            ],
            out_specs=(
                pl.BlockSpec((1, rows, 2 * rank), lambda p, slot: (p, 0, 0)),
                pl.BlockSpec((2, rank, width), lambda p, slot: (p, 0, 0)),
                pl.BlockSpec((1, keys, 2 * rank), lambda p, slot: (p, 0, 0)),
            ),
        ),
        out_shape=(
            struct((pairs, rows, 2 * rank), BF16),
            struct((seqs, rank, width), BF16),
            struct((pairs, keys, 2 * rank), BF16),
        ),
        compiler_params=ALL,
        name="low",
    )(slot_of, panels, panels, activations)
    other_low = lax.ppermute(low_u, "c", SWAP)
    dy_pair = pl.BlockSpec((chips, keys, 2 * rows), lambda p: (0, 0, p))
    mixed = pl.BlockSpec((chips, 1, 2 * keys, 2 * rank), lambda p: (0, p, 0, 0))
    sent = pl.pallas_call(
        project,
        grid=(pairs,),
        in_specs=[
            pl.BlockSpec((1, rows, 2 * rank), lambda p: (p, 0, 0)),
            pl.BlockSpec((1, rows, 2 * rank), lambda p: (p, 0, 0)),
            pl.BlockSpec((1, keys, 2 * rank), lambda p: (p, 0, 0)),
            dy_pair,
        ],
        out_specs=mixed,
        out_shape=struct((chips, pairs, 2 * keys, 2 * rank), BF16),
        compiler_params=STEPS,
        name="project",
    )(low_u, other_low, ups, dy)
    got = lax.all_to_all(sent, "y", 0, 0, tiled=True)

    low_g = pl.pallas_call(
        lower,
        grid=(pairs,),
        in_specs=[mixed, dy_pair],
        out_specs=pl.BlockSpec((2, rank, rows), lambda p: (p, 0, 0)),
        out_shape=struct((seqs, rank, rows), BF16),
        compiler_params=STEPS,
        name="lower",
    )(got, dy)
    other_low = lax.ppermute(low_g, "c", SWAP)
    part_b = pl.pallas_call(
        functools.partial(tally, scale),
        in_specs=[VMEM],
        out_specs=VMEM,
        out_shape=struct((seqs, tall - rank, width), F32),
        compiler_params=PART,
        name="tally",
    )(got)
    low_g, sent = pl.pallas_call(
        functools.partial(combine, scale),
        grid_spec=pltpu.PrefetchScalarGridSpec(
            num_scalar_prefetch=1,
            grid=(seqs,),
            in_specs=[
                pl.BlockSpec((1, rank, rows), lambda s, slot: (s, 0, 0)),
                pl.BlockSpec((1, rank, rows), lambda s, slot: (s, 0, 0)),
                pl.BlockSpec((1, tall - rank, width), lambda s, slot: (s, 0, 0)),
                pl.BlockSpec((rows, width), lambda s, slot: (s, 0)),
            ],
            out_specs=(
                pl.BlockSpec((1, rank, rows), lambda s, slot: (s, 0, 0)),
                pl.BlockSpec((columns, 1, tall + 8, width), lambda s, slot: (0, s, 0, 0)),
            ),
        ),
        out_shape=(
            struct((seqs, rank, rows), BF16),
            struct((columns, seqs, tall + 8, width), BF16),
        ),
        compiler_params=ALL,
        name="combine",
    )(slot_of, low_g, other_low, part_b, activations)
    input_gradient = pl.pallas_call(
        backward,
        grid=(seqs,),
        in_specs=[
            pl.BlockSpec((1, rank, rows), lambda s: (s, 0, 0)),
            pl.BlockSpec((chips, keys, rows), lambda s: (0, 0, s)),
            pl.BlockSpec((chips, keys, rows), lambda s: (0, 0, s)),
            pl.BlockSpec(key_weight.shape, lambda s: (0, 0)),
            pl.BlockSpec((1, rank, width), lambda s: (s, 0, 0)),
        ],
        out_specs=pl.BlockSpec((rows, width), lambda s: (s, 0)),
        out_shape=struct(activations.shape, BF16),
        compiler_params=ALL,
        cost_estimate=pl.CostEstimate(
            flops=2 * activations.shape[0] * width * (key_weight.shape[1] + rank),
            bytes_accessed=2 * (activations.shape[0] + width) * (key_weight.shape[1] + width),
            transcendentals=0,
        ),
        name="backward",
    )(low_g, dy, other_dy, key_weight, down)
    got = lax.all_to_all(sent, "x", 0, 0, tiled=True)

    sent = pl.pallas_call(
        sort,
        out_shape=struct((slots // columns, tall, width), BF16),
        in_specs=[VMEM],
        out_specs=VMEM,
        compiler_params=PART,
        name="sort",
    )(got)
    got = lax.all_to_all(sent, "z", 0, 0, tiled=True)

    grad_a, grad_b = pl.pallas_call(
        finish,
        out_shape=(struct((1, rank, width), F32), struct((1, rank, keys), F32)),
        in_specs=[VMEM],
        out_specs=(VMEM, VMEM),
        compiler_params=PART,
        name="finish",
    )(got)
    return (input_gradient, grad_a, grad_b)


def solution(mesh):
    columns = min(COLUMNS, mesh.shape["dp"] // 2)
    chips = mesh.shape["mp"] // 2
    grid = Mesh(mesh.devices.reshape(-1, columns, chips, 2), ("z", "x", "y", "c"))
    dp, mp = ("z", "x"), ("y", "c")
    in_specs = (
        P(dp, mp),
        P(dp, mp),
        P(mp, None),
        P(dp, None, mp),
        P(dp, None, mp),
        P(dp),
        P(),
    )
    out_specs = (P(dp, mp), P(dp, None, mp), P(dp, None, mp))
    body = functools.partial(local, columns, chips)
    return jax.shard_map(body, mesh=grid, in_specs=in_specs, out_specs=out_specs, check_vma=False)
```

```python
import functools
import math

import jax
import jax.numpy as jnp
from jax import lax
from jax.experimental import pallas as pl
from jax.experimental.pallas import tpu as pltpu
from jax.sharding import Mesh, PartitionSpec as P

ADAPTER_SCALE = 2.0
F32 = jnp.float32
BF16 = jnp.bfloat16
LANES = 128
COLUMNS = 4
SWAP = [(0, 1), (1, 0)]
WHOLE = pltpu.CompilerParams(vmem_limit_bytes=58 * 2**20)
ALL = pltpu.CompilerParams(vmem_limit_bytes=58 * 2**20, dimension_semantics=("arbitrary",))
STEPS = pltpu.CompilerParams(vmem_limit_bytes=24 * 2**20, dimension_semantics=("arbitrary",))
PART = pltpu.CompilerParams(vmem_limit_bytes=24 * 2**20)
VMEM = pl.BlockSpec(memory_space=pltpu.VMEM)
SMEM = pl.BlockSpec(memory_space=pltpu.SMEM)


def left_half(shape):
    return lax.broadcasted_iota(jnp.int32, shape, 1) < LANES // 2


def pack(tall):
    slabs = []
    for i in range(0, tall.shape[0], 16):
        upper, lower = tall[i : i + 8], pltpu.roll(tall[i + 8 : i + 16], LANES // 2, 1)
        slabs.append(jnp.where(left_half(upper.shape), upper, lower))
    return jnp.concatenate(slabs, axis=1)


def unpack(flat, right):
    pieces = []
    for i in range(0, flat.shape[1], LANES):
        slab = flat[:, i : i + LANES]
        turned = pltpu.roll(slab, LANES // 2, 1)
        left = left_half(slab.shape)
        for piece in (turned, slab) if right else (slab, turned):
            pieces.append(jnp.where(left != right, piece, 0.0))
    return jnp.concatenate(pieces, axis=0)


def prepare(down_ref, up_ref, sent_ref):
    up = up_ref[0].astype(F32).T
    packed = pack(jnp.concatenate([up, jnp.zeros_like(up)], axis=1))
    panel = jnp.concatenate([down_ref[0].astype(F32), packed], axis=0).astype(BF16)
    for z in range(sent_ref.shape[0]):
        sent_ref[z] = panel


def select(columns, panel_ref, holder_ref, *refs):
    tenant_refs, (sent_ref, slot_ref, place_ref, table) = refs[:columns], refs[columns:]
    seqs = sent_ref.shape[1]
    for t in range(holder_ref.shape[0]):
        table[holder_ref[t]] = jnp.int32(t)
    here = lax.axis_index("x")
    slot_ref[seqs] = lax.axis_index("c")
    for back, tenant_ref in enumerate(tenant_refs):
        there = lax.rem(here + columns - back, columns)
        for s in range(seqs):
            slot = table[tenant_ref[s]]
            row, column = slot // columns, slot % columns
            if back == 0:
                slot_ref[s] = slot
            place_ref[there * seqs + s] = jnp.where(column == here, row, -1)
            sent_ref[there, s] = panel_ref[row]


def low(slot_ref, panel0_ref, panel1_ref, x_ref, low_ref, down_ref, ups_ref):
    rank = down_ref.shape[1]
    rows = low_ref.shape[1]
    total = ups = 0.0
    for side, panel_ref in enumerate((panel0_ref, panel1_ref)):
        panel = panel_ref[0, 0]
        down = panel[:rank]
        down_ref[side] = down
        blank = jnp.zeros_like(down)
        wide = jnp.concatenate([blank, down] if side else [down, blank], axis=0)
        total = total + lax.dot_general(
            x_ref[side * rows : (side + 1) * rows],
            wide,
            (((1,), (1,)), ((), ())),
            preferred_element_type=F32,
        )
        ups = ups + unpack(panel.astype(F32)[rank:], side == 1)
    low_ref[0] = total.astype(BF16)
    ups_ref[0] = ups.astype(BF16)


def project(slot_ref, low_ref, other_ref, ups_ref, dy_ref, sent_ref):
    rows = low_ref.shape[1]
    chips, _, keys, _ = dy_ref.shape
    low_u = (low_ref[0].astype(F32) + other_ref[0].astype(F32)).astype(BF16)
    dy = dy_ref[...].reshape(chips * keys, 2 * rows)
    parts = [
        jnp.dot(dy[:, side * rows : (side + 1) * rows], low_u, preferred_element_type=F32)
        for side in range(2)
    ]
    part = jnp.where(left_half(parts[0].shape), parts[0], parts[1])
    sent_ref[:, 0, :keys] = part.reshape(chips, keys, LANES).astype(BF16)
    for y in range(chips):
        sent_ref[y, 0, keys:] = ups_ref[0]


def lower(slot_ref, got_ref, dy_ref, low_ref):
    _, rank, rows = low_ref.shape
    chips, _, keys, _ = dy_ref.shape
    ups = got_ref[:, 0, keys:].reshape(chips * keys, LANES)
    dy = dy_ref[...].reshape(chips * keys, 2 * rows)
    for side in range(2):
        both = lax.dot_general(
            ups,
            dy[:, side * rows : (side + 1) * rows],
            (((0,), (0,)), ((), ())),
            preferred_element_type=F32,
        )
        low_ref[side] = both[side * rank : (side + 1) * rank].astype(BF16)


def tally(scale, got_ref, part_ref):
    keys = got_ref.shape[2] // 2
    for pair in range(got_ref.shape[1]):
        total = 0.0
        for y in range(got_ref.shape[0]):
            total = total + got_ref[y, pair, :keys].astype(F32)
        total = scale * total
        part_ref[2 * pair] = pack(total)
        part_ref[2 * pair + 1] = pack(pltpu.roll(total, LANES // 2, 1))


def combine(scale, low_ref, other_ref, part_ref, x_ref, low_g_ref, sent_ref):
    low_g = (low_ref[0].astype(F32) + other_ref[0].astype(F32)).astype(BF16)
    low_g_ref[0] = low_g
    part_a = scale * jnp.dot(low_g, x_ref[...], preferred_element_type=F32)
    panel = jnp.concatenate([part_a, part_ref[0]], axis=0).astype(BF16)
    for x in range(sent_ref.shape[0]):
        sent_ref[x, 0] = panel


def backward(low_ref, dy_ref, weight_ref, down_ref, input_ref):
    frozen = lax.dot_general(
        dy_ref[...], weight_ref[...], (((0,), (1,)), ((), ())), preferred_element_type=F32
    )
    update = lax.dot_general(
        low_ref[0], down_ref[0], (((0,), (0,)), ((), ())), preferred_element_type=F32
    )
    input_ref[...] = (frozen + ADAPTER_SCALE * update).astype(BF16)


def sort(place_ref, got_ref, sent_ref, total):
    columns, seqs = got_ref.shape[:2]
    total[...] = jnp.zeros_like(total)
    for x in range(columns):
        for s in range(seqs):
            place = place_ref[x * seqs + s]

            @pl.when(place >= 0)
            def _():
                total[place] += got_ref[x, s].astype(F32)

    sent_ref[...] = total[...].astype(BF16)


def finish(got_ref, down_ref, up_ref):
    rank = down_ref.shape[1]
    total = got_ref[0].astype(F32)
    for p in range(1, got_ref.shape[0]):
        total = total + got_ref[p].astype(F32)
    down_ref[0] = total[:rank]
    up_ref[0] = unpack(total[rank:], False)[:, :rank].T


def local(
    columns,
    chips,
    activations,
    cotangent,
    key_weight,
    adapter_down,
    adapter_up,
    sequence_tenant,
    slot_holder_tenant,
):
    seqs = sequence_tenant.shape[0]
    rows = activations.shape[0] // seqs
    width = activations.shape[1]
    keys = cotangent.shape[1]
    rank = adapter_down.shape[1]
    slots = slot_holder_tenant.shape[0]
    tall = rank + rank * keys // width
    scale = ADAPTER_SCALE / math.sqrt(seqs * rows)
    struct = jax.ShapeDtypeStruct

    dy = lax.all_gather(cotangent.T, ("y", "c"), axis=0, tiled=True)
    dy_halves = dy.reshape(chips, 2, keys, dy.shape[1])

    tenants = [sequence_tenant] + [
        lax.ppermute(sequence_tenant, "x", [(x, (x + d) % columns) for x in range(columns)])
        for d in range(1, columns)
    ]
    sent = pl.pallas_call(
        prepare,
        out_shape=struct((slots // columns, tall, width), BF16),
        in_specs=[VMEM, VMEM],
        out_specs=VMEM,
        compiler_params=WHOLE,
        name="prepare",
    )(adapter_down, adapter_up)
    panels = lax.all_to_all(sent, "z", 0, 0, tiled=True)
    sent, slot_of, place_of = pl.pallas_call(
        functools.partial(select, columns),
        out_shape=(
            struct((columns, seqs, tall, width), BF16),
            struct((seqs + 1,), jnp.int32),
            struct((columns * seqs,), jnp.int32),
        ),
        in_specs=[VMEM] + [SMEM] * (1 + columns),
        out_specs=(VMEM, SMEM, SMEM),
        scratch_shapes=[pltpu.SMEM((slots,), jnp.int32)],
        compiler_params=PART,
        name="select",
    )(panels, slot_holder_tenant, *tenants)
    panels = lax.all_to_all(sent, "x", 0, 0, tiled=True)

    pairs = seqs // 2
    low_u, down, ups = pl.pallas_call(
        low,
        grid_spec=pltpu.PrefetchScalarGridSpec(
            num_scalar_prefetch=1,
            grid=(pairs,),
            in_specs=[
                pl.BlockSpec(
                    (1, 1, tall, width),
                    lambda p, slot: (slot[2 * p] % columns, 2 * p, 0, 0),
                ),
                pl.BlockSpec(
                    (1, 1, tall, width),
                    lambda p, slot: (slot[2 * p + 1] % columns, 2 * p + 1, 0, 0),
                ),
                pl.BlockSpec((2 * rows, width), lambda p, slot: (p, 0)),
            ],
            out_specs=(
                pl.BlockSpec((1, rows, 2 * rank), lambda p, slot: (p, 0, 0)),
                pl.BlockSpec((2, rank, width), lambda p, slot: (p, 0, 0)),
                pl.BlockSpec((1, keys, 2 * rank), lambda p, slot: (p, 0, 0)),
            ),
        ),
        out_shape=(
            struct((pairs, rows, 2 * rank), BF16),
            struct((seqs, rank, width), BF16),
            struct((pairs, keys, 2 * rank), BF16),
        ),
        compiler_params=ALL,
        name="low",
    )(slot_of, panels, panels, activations)
    other_low = lax.ppermute(low_u, "c", SWAP)
    dy_pair = pl.BlockSpec(
        (chips, 1, keys, 2 * rows), lambda p, slot: (0, slot[seqs], 0, p)
    )
    mixed = pl.BlockSpec((chips, 1, 2 * keys, 2 * rank), lambda p, slot: (0, p, 0, 0))
    sent = pl.pallas_call(
        project,
        grid_spec=pltpu.PrefetchScalarGridSpec(
            num_scalar_prefetch=1,
            grid=(pairs,),
            in_specs=[
                pl.BlockSpec((1, rows, 2 * rank), lambda p, slot: (p, 0, 0)),
                pl.BlockSpec((1, rows, 2 * rank), lambda p, slot: (p, 0, 0)),
                pl.BlockSpec((1, keys, 2 * rank), lambda p, slot: (p, 0, 0)),
                dy_pair,
            ],
            out_specs=mixed,
        ),
        out_shape=struct((chips, pairs, 2 * keys, 2 * rank), BF16),
        compiler_params=ALL,
        name="project",
    )(slot_of, low_u, other_low, ups, dy_halves)
    got = lax.all_to_all(sent, "y", 0, 0, tiled=True)

    low_g = pl.pallas_call(
        lower,
        grid_spec=pltpu.PrefetchScalarGridSpec(
            num_scalar_prefetch=1,
            grid=(pairs,),
            in_specs=[mixed, dy_pair],
            out_specs=pl.BlockSpec((2, rank, rows), lambda p, slot: (p, 0, 0)),
        ),
        out_shape=struct((seqs, rank, rows), BF16),
        compiler_params=STEPS,
        name="lower",
    )(slot_of, got, dy_halves)
    other_low = lax.ppermute(low_g, "c", SWAP)
    part_b = pl.pallas_call(
        functools.partial(tally, scale),
        in_specs=[VMEM],
        out_specs=VMEM,
        out_shape=struct((seqs, tall - rank, width), F32),
        compiler_params=PART,
        name="tally",
    )(got)
    one = pl.BlockSpec((1, rank, rows), lambda s: (s, 0, 0))
    low_g, sent = pl.pallas_call(
        functools.partial(combine, scale),
        grid=(seqs,),
        in_specs=[
            one,
            one,
            pl.BlockSpec((1, tall - rank, width), lambda s: (s, 0, 0)),
            pl.BlockSpec((rows, width), lambda s: (s, 0)),
        ],
        out_specs=(one, pl.BlockSpec((columns, 1, tall, width), lambda s: (0, s, 0, 0))),
        out_shape=(
            struct((seqs, rank, rows), BF16),
            struct((columns, seqs, tall, width), BF16),
        ),
        compiler_params=STEPS,
        name="combine",
    )(low_g, other_low, part_b, activations)
    input_gradient = pl.pallas_call(
        backward,
        grid=(seqs,),
        in_specs=[
            one,
            pl.BlockSpec((dy.shape[0], rows), lambda s: (0, s)),
            pl.BlockSpec(key_weight.shape, lambda s: (0, 0)),
            pl.BlockSpec((1, rank, width), lambda s: (s, 0, 0)),
        ],
        out_specs=pl.BlockSpec((rows, width), lambda s: (s, 0)),
        out_shape=struct(activations.shape, BF16),
        compiler_params=ALL,
        cost_estimate=pl.CostEstimate(
            flops=2 * activations.shape[0] * width * (key_weight.shape[1] + rank),
            bytes_accessed=2 * (activations.shape[0] + width) * (key_weight.shape[1] + width),
            transcendentals=0,
        ),
        name="backward",
    )(low_g, dy, key_weight, down)
    got = lax.all_to_all(sent, "x", 0, 0, tiled=True)

    sent = pl.pallas_call(
        sort,
        out_shape=struct((slots // columns, tall, width), BF16),
        in_specs=[SMEM, VMEM],
        out_specs=VMEM,
        scratch_shapes=[pltpu.VMEM((slots // columns, tall, width), F32)],
        compiler_params=PART,
        name="sort",
    )(place_of, got)
    got = lax.all_to_all(sent, "z", 0, 0, tiled=True)

    grad_a, grad_b = pl.pallas_call(
        finish,
        out_shape=(struct((1, rank, width), F32), struct((1, rank, keys), F32)),
        in_specs=[VMEM],
        out_specs=(VMEM, VMEM),
        compiler_params=PART,
        name="finish",
    )(got)
    return (input_gradient, grad_a, grad_b)


def solution(mesh):
    columns = min(COLUMNS, mesh.shape["dp"] // 2)
    chips = mesh.shape["mp"] // 2
    grid = Mesh(mesh.devices.reshape(-1, columns, chips, 2), ("z", "x", "y", "c"))
    dp, mp = ("z", "x"), ("y", "c")
    in_specs = (
        P(dp, mp),
        P(dp, mp),
        P(mp, None),
        P(dp, None, mp),
        P(dp, None, mp),
        P(dp),
        P(),
    )
    out_specs = (P(dp, mp), P(dp, None, mp), P(dp, None, mp))
    body = functools.partial(local, columns, chips)
    return jax.shard_map(body, mesh=grid, in_specs=in_specs, out_specs=out_specs, check_vma=False)
```

```python
import functools
import math

import jax
import jax.numpy as jnp
from jax import lax
from jax.experimental import pallas as pl
from jax.experimental.pallas import tpu as pltpu
from jax.sharding import Mesh, PartitionSpec as P

ADAPTER_SCALE = 2.0
F32 = jnp.float32
BF16 = jnp.bfloat16
LANES = 128
COLUMNS = 4
SWAP = [(0, 1), (1, 0)]
WHOLE = pltpu.CompilerParams(vmem_limit_bytes=58 * 2**20)
ALL = pltpu.CompilerParams(vmem_limit_bytes=58 * 2**20, dimension_semantics=("arbitrary",))
STEPS = pltpu.CompilerParams(vmem_limit_bytes=24 * 2**20, dimension_semantics=("arbitrary",))
PART = pltpu.CompilerParams(vmem_limit_bytes=24 * 2**20)
VMEM = pl.BlockSpec(memory_space=pltpu.VMEM)
SMEM = pl.BlockSpec(memory_space=pltpu.SMEM)


def left_half(shape):
    return lax.broadcasted_iota(jnp.int32, shape, 1) < LANES // 2


def pack(tall):
    slabs = []
    for i in range(0, tall.shape[0], 16):
        upper, lower = tall[i : i + 8], pltpu.roll(tall[i + 8 : i + 16], LANES // 2, 1)
        slabs.append(jnp.where(left_half(upper.shape), upper, lower))
    return jnp.concatenate(slabs, axis=1)


def unpack(flat, right):
    pieces = []
    for i in range(0, flat.shape[1], LANES):
        slab = flat[:, i : i + LANES]
        turned = pltpu.roll(slab, LANES // 2, 1)
        left = left_half(slab.shape)
        for piece in (turned, slab) if right else (slab, turned):
            pieces.append(jnp.where(left != right, piece, 0.0))
    return jnp.concatenate(pieces, axis=0)


def prepare(down_ref, up_ref, sent_ref):
    up = up_ref[0].astype(F32).T
    packed = pack(jnp.concatenate([up, jnp.zeros_like(up)], axis=1))
    panel = jnp.concatenate([down_ref[0].astype(F32), packed], axis=0).astype(BF16)
    for z in range(sent_ref.shape[0]):
        sent_ref[z] = panel


def select(columns, panel_ref, holder_ref, *refs):
    tenant_refs, (sent_ref, slot_ref, place_ref, table) = refs[:columns], refs[columns:]
    seqs = sent_ref.shape[1]
    for t in range(holder_ref.shape[0]):
        table[holder_ref[t]] = jnp.int32(t)
    here = lax.axis_index("x")
    slot_ref[seqs] = lax.axis_index("c")
    for back, tenant_ref in enumerate(tenant_refs):
        there = lax.rem(here + columns - back, columns)
        for s in range(seqs):
            slot = table[tenant_ref[s]]
            row, column = slot // columns, slot % columns
            if back == 0:
                slot_ref[s] = slot
            place_ref[there * seqs + s] = jnp.where(column == here, row, -1)
            sent_ref[there, s] = panel_ref[row]


def low(slot_ref, panel0_ref, panel1_ref, x_ref, _, low_ref, ups_ref):
    rows, rank = low_ref.shape[1], low_ref.shape[2] // 2
    total = ups = 0.0
    for side, panel_ref in enumerate((panel0_ref, panel1_ref)):
        panel = panel_ref[0, 0]
        down = panel[:rank]
        blank = jnp.zeros_like(down)
        wide = jnp.concatenate([blank, down] if side else [down, blank], axis=0)
        total = total + lax.dot_general(
            x_ref[side * rows : (side + 1) * rows],
            wide,
            (((1,), (1,)), ((), ())),
            preferred_element_type=F32,
        )
        ups = ups + unpack(panel.astype(F32)[rank:], side == 1)
    low_ref[0] = total.astype(BF16)
    ups_ref[0] = ups.astype(BF16)


def project(slot_ref, low_ref, other_ref, ups_ref, dy_ref, sent_ref):
    rows = low_ref.shape[1]
    chips, _, keys, _ = dy_ref.shape
    low_u = (low_ref[0].astype(F32) + other_ref[0].astype(F32)).astype(BF16)
    dy = dy_ref[...].reshape(chips * keys, 2 * rows)
    parts = [
        jnp.dot(dy[:, side * rows : (side + 1) * rows], low_u, preferred_element_type=F32)
        for side in range(2)
    ]
    part = jnp.where(left_half(parts[0].shape), parts[0], parts[1])
    sent_ref[:, 0, :keys] = part.reshape(chips, keys, LANES).astype(BF16)
    for y in range(chips):
        sent_ref[y, 0, keys:] = ups_ref[0]


def lower(slot_ref, got_ref, dy_ref, low_ref):
    _, rank, rows = low_ref.shape
    chips, _, keys, _ = dy_ref.shape
    ups = got_ref[:, 0, keys:].reshape(chips * keys, LANES)
    dy = dy_ref[...].reshape(chips * keys, 2 * rows)
    for side in range(2):
        both = lax.dot_general(
            ups,
            dy[:, side * rows : (side + 1) * rows],
            (((0,), (0,)), ((), ())),
            preferred_element_type=F32,
        )
        low_ref[side] = both[side * rank : (side + 1) * rank].astype(BF16)


def tally(scale, got_ref, part_ref):
    keys = got_ref.shape[2] // 2
    for pair in range(got_ref.shape[1]):
        total = 0.0
        for y in range(got_ref.shape[0]):
            total = total + got_ref[y, pair, :keys].astype(F32)
        total = scale * total
        part_ref[2 * pair] = pack(total)
        part_ref[2 * pair + 1] = pack(pltpu.roll(total, LANES // 2, 1))


def combine(scale, low_ref, other_ref, part_ref, x_ref, low_g_ref, sent_ref):
    low_g = (low_ref[0].astype(F32) + other_ref[0].astype(F32)).astype(BF16)
    low_g_ref[0] = low_g
    part_a = scale * jnp.dot(low_g, x_ref[...], preferred_element_type=F32)
    panel = jnp.concatenate([part_a, part_ref[0]], axis=0).astype(BF16)
    for x in range(sent_ref.shape[0]):
        sent_ref[x, 0] = panel


def backward(slot_ref, low_ref, dy_ref, weight_ref, panel_ref, input_ref):
    frozen = lax.dot_general(
        dy_ref[...], weight_ref[...], (((0,), (1,)), ((), ())), preferred_element_type=F32
    )
    update = lax.dot_general(
        low_ref[0],
        panel_ref[0, 0][: low_ref.shape[1]],
        (((0,), (0,)), ((), ())),
        preferred_element_type=F32,
    )
    input_ref[...] = (frozen + ADAPTER_SCALE * update).astype(BF16)


def sort(place_ref, got_ref, sent_ref, total):
    columns, seqs = got_ref.shape[:2]
    total[...] = jnp.zeros_like(total)
    for x in range(columns):
        for s in range(seqs):
            place = place_ref[x * seqs + s]

            @pl.when(place >= 0)
            def _():
                total[place] += got_ref[x, s].astype(F32)

    sent_ref[...] = total[...].astype(BF16)


def finish(got_ref, down_ref, up_ref):
    rank = down_ref.shape[1]
    total = got_ref[0].astype(F32)
    for p in range(1, got_ref.shape[0]):
        total = total + got_ref[p].astype(F32)
    down_ref[0] = total[:rank]
    up_ref[0] = unpack(total[rank:], False)[:, :rank].T


def local(
    columns,
    chips,
    activations,
    cotangent,
    key_weight,
    adapter_down,
    adapter_up,
    sequence_tenant,
    slot_holder_tenant,
):
    seqs = sequence_tenant.shape[0]
    rows = activations.shape[0] // seqs
    width = activations.shape[1]
    keys = cotangent.shape[1]
    rank = adapter_down.shape[1]
    slots = slot_holder_tenant.shape[0]
    tall = rank + rank * keys // width
    scale = ADAPTER_SCALE / math.sqrt(seqs * rows)
    struct = jax.ShapeDtypeStruct

    dy = lax.all_gather(cotangent.T, ("y", "c"), axis=0, tiled=True)
    dy_halves = dy.reshape(chips, 2, keys, dy.shape[1])

    tenants = [sequence_tenant] + [
        lax.ppermute(sequence_tenant, "x", [(x, (x + d) % columns) for x in range(columns)])
        for d in range(1, columns)
    ]
    sent = pl.pallas_call(
        prepare,
        out_shape=struct((slots // columns, tall, width), BF16),
        in_specs=[VMEM, VMEM],
        out_specs=VMEM,
        compiler_params=WHOLE,
        name="prepare",
    )(adapter_down, adapter_up)
    panels = lax.all_to_all(sent, "z", 0, 0, tiled=True)
    sent, slot_of, place_of = pl.pallas_call(
        functools.partial(select, columns),
        out_shape=(
            struct((columns, seqs, tall, width), BF16),
            struct((seqs + 1,), jnp.int32),
            struct((columns * seqs,), jnp.int32),
        ),
        in_specs=[VMEM] + [SMEM] * (1 + columns),
        out_specs=(VMEM, SMEM, SMEM),
        scratch_shapes=[pltpu.SMEM((slots,), jnp.int32)],
        compiler_params=PART,
        name="select",
    )(panels, slot_holder_tenant, *tenants)
    panels = lax.all_to_all(sent, "x", 0, 0, tiled=True)

    pairs = seqs // 2
    low_u, ups = pl.pallas_call(
        low,
        grid_spec=pltpu.PrefetchScalarGridSpec(
            num_scalar_prefetch=1,
            grid=(pairs,),
            in_specs=[
                pl.BlockSpec(
                    (1, 1, tall, width),
                    lambda p, slot: (slot[2 * p] % columns, 2 * p, 0, 0),
                ),
                pl.BlockSpec(
                    (1, 1, tall, width),
                    lambda p, slot: (slot[2 * p + 1] % columns, 2 * p + 1, 0, 0),
                ),
                pl.BlockSpec((2 * rows, width), lambda p, slot: (p, 0)),
                pl.BlockSpec(memory_space=pl.ANY),
            ],
            out_specs=(
                pl.BlockSpec((1, rows, 2 * rank), lambda p, slot: (p, 0, 0)),
                pl.BlockSpec((1, keys, 2 * rank), lambda p, slot: (p, 0, 0)),
            ),
        ),
        out_shape=(
            struct((pairs, rows, 2 * rank), BF16),
            struct((pairs, keys, 2 * rank), BF16),
        ),
        compiler_params=ALL,
        name="low",
    )(slot_of, panels, panels, activations, dy)
    other_low = lax.ppermute(low_u, "c", SWAP)
    dy_pair = pl.BlockSpec(
        (chips, 1, keys, 2 * rows), lambda p, slot: (0, slot[seqs], 0, p)
    )
    mixed = pl.BlockSpec((chips, 1, 2 * keys, 2 * rank), lambda p, slot: (0, p, 0, 0))
    sent = pl.pallas_call(
        project,
        grid_spec=pltpu.PrefetchScalarGridSpec(
            num_scalar_prefetch=1,
            grid=(pairs,),
            in_specs=[
                pl.BlockSpec((1, rows, 2 * rank), lambda p, slot: (p, 0, 0)),
                pl.BlockSpec((1, rows, 2 * rank), lambda p, slot: (p, 0, 0)),
                pl.BlockSpec((1, keys, 2 * rank), lambda p, slot: (p, 0, 0)),
                dy_pair,
            ],
            out_specs=mixed,
        ),
        out_shape=struct((chips, pairs, 2 * keys, 2 * rank), BF16),
        compiler_params=STEPS,
        name="project",
    )(slot_of, low_u, other_low, ups, dy_halves)
    got = lax.all_to_all(sent, "y", 0, 0, tiled=True)

    low_g = pl.pallas_call(
        lower,
        grid_spec=pltpu.PrefetchScalarGridSpec(
            num_scalar_prefetch=1,
            grid=(pairs,),
            in_specs=[mixed, dy_pair],
            out_specs=pl.BlockSpec((2, rank, rows), lambda p, slot: (p, 0, 0)),
        ),
        out_shape=struct((seqs, rank, rows), BF16),
        compiler_params=STEPS,
        name="lower",
    )(slot_of, got, dy_halves)
    other_low = lax.ppermute(low_g, "c", SWAP)
    part_b = pl.pallas_call(
        functools.partial(tally, scale),
        in_specs=[VMEM],
        out_specs=VMEM,
        out_shape=struct((seqs, tall - rank, width), F32),
        compiler_params=PART,
        name="tally",
    )(got)
    one = pl.BlockSpec((1, rank, rows), lambda s: (s, 0, 0))
    low_g, sent = pl.pallas_call(
        functools.partial(combine, scale),
        grid=(seqs,),
        in_specs=[
            one,
            one,
            pl.BlockSpec((1, tall - rank, width), lambda s: (s, 0, 0)),
            pl.BlockSpec((rows, width), lambda s: (s, 0)),
        ],
        out_specs=(one, pl.BlockSpec((columns, 1, tall, width), lambda s: (0, s, 0, 0))),
        out_shape=(
            struct((seqs, rank, rows), BF16),
            struct((columns, seqs, tall, width), BF16),
        ),
        compiler_params=STEPS,
        name="combine",
    )(low_g, other_low, part_b, activations)
    input_gradient = pl.pallas_call(
        backward,
        grid_spec=pltpu.PrefetchScalarGridSpec(
            num_scalar_prefetch=1,
            grid=(seqs,),
            in_specs=[
                pl.BlockSpec((1, rank, rows), lambda s, slot: (s, 0, 0)),
                pl.BlockSpec((dy.shape[0], rows), lambda s, slot: (0, s)),
                pl.BlockSpec(key_weight.shape, lambda s, slot: (0, 0)),
                pl.BlockSpec((1, 1, tall, width), lambda s, slot: (slot[s] % columns, s, 0, 0)),
            ],
            out_specs=pl.BlockSpec((rows, width), lambda s, slot: (s, 0)),
        ),
        out_shape=struct(activations.shape, BF16),
        compiler_params=ALL,
        cost_estimate=pl.CostEstimate(
            flops=2 * activations.shape[0] * width * (key_weight.shape[1] + rank),
            bytes_accessed=2 * (activations.shape[0] + width) * (key_weight.shape[1] + width),
            transcendentals=0,
        ),
        name="backward",
    )(slot_of, low_g, dy, key_weight, panels)
    got = lax.all_to_all(sent, "x", 0, 0, tiled=True)

    sent = pl.pallas_call(
        sort,
        out_shape=struct((slots // columns, tall, width), BF16),
        in_specs=[SMEM, VMEM],
        out_specs=VMEM,
        scratch_shapes=[pltpu.VMEM((slots // columns, tall, width), F32)],
        compiler_params=PART,
        name="sort",
    )(place_of, got)
    got = lax.all_to_all(sent, "z", 0, 0, tiled=True)

    grad_a, grad_b = pl.pallas_call(
        finish,
        out_shape=(struct((1, rank, width), F32), struct((1, rank, keys), F32)),
        in_specs=[VMEM],
        out_specs=(VMEM, VMEM),
        compiler_params=PART,
        name="finish",
    )(got)
    return (input_gradient, grad_a, grad_b)


def solution(mesh):
    columns = min(COLUMNS, mesh.shape["dp"] // 2)
    chips = mesh.shape["mp"] // 2
    grid = Mesh(mesh.devices.reshape(-1, columns, chips, 2), ("z", "x", "y", "c"))
    dp, mp = ("z", "x"), ("y", "c")
    in_specs = (
        P(dp, mp),
        P(dp, mp),
        P(mp, None),
        P(dp, None, mp),
        P(dp, None, mp),
        P(dp),
        P(),
    )
    out_specs = (P(dp, mp), P(dp, None, mp), P(dp, None, mp))
    body = functools.partial(local, columns, chips)
    return jax.shard_map(body, mesh=grid, in_specs=in_specs, out_specs=out_specs, check_vma=False)
```

```python
import functools
import math

import jax
import jax.numpy as jnp
from jax import lax
from jax.experimental import pallas as pl
from jax.experimental.pallas import tpu as pltpu
from jax.sharding import Mesh, PartitionSpec as P

ADAPTER_SCALE = 2.0
F32 = jnp.float32
BF16 = jnp.bfloat16
LANES = 128
COLUMNS = 4
SWAP = [(0, 1), (1, 0)]
WHOLE = pltpu.CompilerParams(vmem_limit_bytes=58 * 2**20)
ALL = pltpu.CompilerParams(vmem_limit_bytes=58 * 2**20, dimension_semantics=("arbitrary",))
STEPS = pltpu.CompilerParams(vmem_limit_bytes=24 * 2**20, dimension_semantics=("arbitrary",))
PART = pltpu.CompilerParams(vmem_limit_bytes=24 * 2**20)
VMEM = pl.BlockSpec(memory_space=pltpu.VMEM)
SMEM = pl.BlockSpec(memory_space=pltpu.SMEM)


def left_half(shape):
    return lax.broadcasted_iota(jnp.int32, shape, 1) < LANES // 2


def pack(tall):
    slabs = []
    for i in range(0, tall.shape[0], 16):
        upper, lower = tall[i : i + 8], pltpu.roll(tall[i + 8 : i + 16], LANES // 2, 1)
        slabs.append(jnp.where(left_half(upper.shape), upper, lower))
    return jnp.concatenate(slabs, axis=1)


def unpack(flat, right):
    pieces = []
    for i in range(0, flat.shape[1], LANES):
        slab = flat[:, i : i + LANES]
        turned = pltpu.roll(slab, LANES // 2, 1)
        left = left_half(slab.shape)
        for piece in (turned, slab) if right else (slab, turned):
            pieces.append(jnp.where(left != right, piece, 0.0))
    return jnp.concatenate(pieces, axis=0)


def prepare(down_ref, up_ref, sent_ref):
    up = up_ref[0].astype(F32).T
    packed = pack(jnp.concatenate([up, jnp.zeros_like(up)], axis=1))
    panel = jnp.concatenate([down_ref[0].astype(F32), packed], axis=0).astype(BF16)
    for z in range(sent_ref.shape[0]):
        sent_ref[z] = panel


def select(columns, panel_ref, holder_ref, *refs):
    tenant_refs, (sent_ref, slot_ref, place_ref, table) = refs[:columns], refs[-4:]
    seqs = sent_ref.shape[1]
    for t in range(holder_ref.shape[0]):
        table[holder_ref[t]] = jnp.int32(t)
    here = lax.axis_index("x")
    for back, tenant_ref in enumerate(tenant_refs):
        there = lax.rem(here + columns - back, columns)
        for s in range(seqs):
            slot = table[tenant_ref[s]]
            row, column = slot // columns, slot % columns
            if back == 0:
                slot_ref[s] = slot
            place_ref[there * seqs + s] = jnp.where(column == here, row, -1)
            sent_ref[there, s] = panel_ref[row]


def stack(chips, *refs):
    slices, (out_ref, sem) = refs[:chips], refs[chips:]
    here = lax.axis_index("y")
    copies = []
    for back, ref in enumerate(slices):
        there = lax.rem(here + chips - back, chips)
        copies.append(pltpu.make_async_copy(ref, out_ref.at[there], sem.at[back]))
        copies[-1].start()
    for copy in copies:
        copy.wait()


def low(slot_ref, panel0_ref, panel1_ref, x_ref, low_ref, ups_ref):
    rows, rank = low_ref.shape[1], low_ref.shape[2] // 2
    total = ups = 0.0
    for side, panel_ref in enumerate((panel0_ref, panel1_ref)):
        panel = panel_ref[0, 0]
        down = panel[:rank]
        blank = jnp.zeros_like(down)
        wide = jnp.concatenate([blank, down] if side else [down, blank], axis=0)
        total = total + lax.dot_general(
            x_ref[side * rows : (side + 1) * rows],
            wide,
            (((1,), (1,)), ((), ())),
            preferred_element_type=F32,
        )
        ups = ups + unpack(panel.astype(F32)[rank:], side == 1)
    low_ref[0] = total.astype(BF16)
    ups_ref[0] = ups.astype(BF16)


def project(low_ref, other_ref, ups_ref, dy_ref, sent_ref):
    rows = low_ref.shape[1]
    chips, keys, _ = dy_ref.shape
    low_u = (low_ref[0].astype(F32) + other_ref[0].astype(F32)).astype(BF16)
    dy = dy_ref[...].reshape(chips * keys, 2 * rows)
    parts = [
        jnp.dot(dy[:, side * rows : (side + 1) * rows], low_u, preferred_element_type=F32)
        for side in range(2)
    ]
    part = jnp.where(left_half(parts[0].shape), parts[0], parts[1])
    sent_ref[:, 0, :keys] = part.reshape(chips, keys, LANES).astype(BF16)
    for y in range(chips):
        sent_ref[y, 0, keys:] = ups_ref[0]


def lower(got_ref, dy_ref, low_ref):
    _, rank, rows = low_ref.shape
    chips, keys, _ = dy_ref.shape
    ups = got_ref[:, 0, keys:].reshape(chips * keys, LANES)
    dy = dy_ref[...].reshape(chips * keys, 2 * rows)
    for side in range(2):
        both = lax.dot_general(
            ups,
            dy[:, side * rows : (side + 1) * rows],
            (((0,), (0,)), ((), ())),
            preferred_element_type=F32,
        )
        low_ref[side] = both[side * rank : (side + 1) * rank].astype(BF16)


def tally(scale, got_ref, part_ref):
    keys = got_ref.shape[2] // 2
    for pair in range(got_ref.shape[1]):
        total = 0.0
        for y in range(got_ref.shape[0]):
            total = total + got_ref[y, pair, :keys].astype(F32)
        total = scale * total
        part_ref[2 * pair] = pack(total)
        part_ref[2 * pair + 1] = pack(pltpu.roll(total, LANES // 2, 1))


def combine(scale, low_ref, other_ref, part_ref, x_ref, low_g_ref, sent_ref):
    low_g = (low_ref[0].astype(F32) + other_ref[0].astype(F32)).astype(BF16)
    low_g_ref[0] = low_g
    part_a = scale * jnp.dot(low_g, x_ref[...], preferred_element_type=F32)
    panel = jnp.concatenate([part_a, part_ref[0]], axis=0).astype(BF16)
    for x in range(sent_ref.shape[0]):
        sent_ref[x, 0] = panel


def backward(slot_ref, low_ref, dy_ref, other_ref, weight_ref, panel_ref, input_ref):
    first = lax.axis_index("c") == 0
    dy, other = dy_ref[...], other_ref[...]
    both = jnp.concatenate(
        [jnp.where(first, dy, other), jnp.where(first, other, dy)], axis=1
    )
    frozen = lax.dot_general(
        both.reshape(-1, dy.shape[2]),
        weight_ref[...],
        (((0,), (1,)), ((), ())),
        preferred_element_type=F32,
    )
    update = lax.dot_general(
        low_ref[0],
        panel_ref[0, 0][: low_ref.shape[1]],
        (((0,), (0,)), ((), ())),
        preferred_element_type=F32,
    )
    input_ref[...] = (frozen + ADAPTER_SCALE * update).astype(BF16)


def sort(place_ref, got_ref, sent_ref, total):
    columns, seqs = got_ref.shape[:2]
    total[...] = jnp.zeros_like(total)
    for x in range(columns):
        for s in range(seqs):
            place = place_ref[x * seqs + s]

            @pl.when(place >= 0)
            def _():
                total[place] += got_ref[x, s].astype(F32)

    sent_ref[...] = total[...].astype(BF16)


def finish(got_ref, down_ref, up_ref):
    rank = down_ref.shape[1]
    total = got_ref[0].astype(F32)
    for p in range(1, got_ref.shape[0]):
        total = total + got_ref[p].astype(F32)
    down_ref[0] = total[:rank]
    up_ref[0] = unpack(total[rank:], False)[:, :rank].T


def local(
    columns,
    chips,
    activations,
    cotangent,
    key_weight,
    adapter_down,
    adapter_up,
    sequence_tenant,
    slot_holder_tenant,
):
    seqs = sequence_tenant.shape[0]
    rows = activations.shape[0] // seqs
    width = activations.shape[1]
    keys = cotangent.shape[1]
    rank = adapter_down.shape[1]
    slots = slot_holder_tenant.shape[0]
    tall = rank + rank * keys // width
    scale = ADAPTER_SCALE / math.sqrt(seqs * rows)
    struct = jax.ShapeDtypeStruct

    own = cotangent.T
    slices = [own] + [
        lax.ppermute(own, "y", [(y, (y + d) % chips) for y in range(chips)])
        for d in range(1, chips)
    ]
    near = [slices[d] for d in sorted({1, chips - 1})]
    anywhere = pl.BlockSpec(memory_space=pl.ANY)
    dy = pl.pallas_call(
        functools.partial(stack, chips),
        out_shape=struct((chips,) + own.shape, BF16),
        in_specs=[anywhere] * chips,
        out_specs=anywhere,
        scratch_shapes=[pltpu.SemaphoreType.DMA((chips,))],
        compiler_params=PART,
        name="stack",
    )(*slices)
    other_dy = lax.ppermute(dy, "c", SWAP)

    tenants = [sequence_tenant] + [
        lax.ppermute(sequence_tenant, "x", [(x, (x + d) % columns) for x in range(columns)])
        for d in range(1, columns)
    ]
    sent = pl.pallas_call(
        prepare,
        out_shape=struct((slots // columns, tall, width), BF16),
        in_specs=[VMEM, VMEM],
        out_specs=VMEM,
        compiler_params=WHOLE,
        name="prepare",
    )(adapter_down, adapter_up)
    panels = lax.all_to_all(sent, "z", 0, 0, tiled=True)
    sent, slot_of, place_of = pl.pallas_call(
        functools.partial(select, columns),
        out_shape=(
            struct((columns, seqs, tall, width), BF16),
            struct((seqs,), jnp.int32),
            struct((columns * seqs,), jnp.int32),
        ),
        in_specs=[VMEM] + [SMEM] * (1 + columns) + [anywhere] * len(near),
        out_specs=(VMEM, SMEM, SMEM),
        scratch_shapes=[pltpu.SMEM((slots,), jnp.int32)],
        compiler_params=PART,
        name="select",
    )(panels, slot_holder_tenant, *tenants, *near)
    panels = lax.all_to_all(sent, "x", 0, 0, tiled=True)

    pairs = seqs // 2
    low_u, ups = pl.pallas_call(
        low,
        grid_spec=pltpu.PrefetchScalarGridSpec(
            num_scalar_prefetch=1,
            grid=(pairs,),
            in_specs=[
                pl.BlockSpec(
                    (1, 1, tall, width),
                    lambda p, slot: (slot[2 * p] % columns, 2 * p, 0, 0),
                ),
                pl.BlockSpec(
                    (1, 1, tall, width),
                    lambda p, slot: (slot[2 * p + 1] % columns, 2 * p + 1, 0, 0),
                ),
                pl.BlockSpec((2 * rows, width), lambda p, slot: (p, 0)),
            ],
            out_specs=(
                pl.BlockSpec((1, rows, 2 * rank), lambda p, slot: (p, 0, 0)),
                pl.BlockSpec((1, keys, 2 * rank), lambda p, slot: (p, 0, 0)),
            ),
        ),
        out_shape=(
            struct((pairs, rows, 2 * rank), BF16),
            struct((pairs, keys, 2 * rank), BF16),
        ),
        compiler_params=ALL,
        name="low",
    )(slot_of, panels, panels, activations)
    other_low = lax.ppermute(low_u, "c", SWAP)
    dy_pair = pl.BlockSpec((chips, keys, 2 * rows), lambda p: (0, 0, p))
    mixed = pl.BlockSpec((chips, 1, 2 * keys, 2 * rank), lambda p: (0, p, 0, 0))
    sent = pl.pallas_call(
        project,
        grid=(pairs,),
        in_specs=[
            pl.BlockSpec((1, rows, 2 * rank), lambda p: (p, 0, 0)),
            pl.BlockSpec((1, rows, 2 * rank), lambda p: (p, 0, 0)),
            pl.BlockSpec((1, keys, 2 * rank), lambda p: (p, 0, 0)),
            dy_pair,
        ],
        out_specs=mixed,
        out_shape=struct((chips, pairs, 2 * keys, 2 * rank), BF16),
        compiler_params=STEPS,
        name="project",
    )(low_u, other_low, ups, dy)
    got = lax.all_to_all(sent, "y", 0, 0, tiled=True)

    low_g = pl.pallas_call(
        lower,
        grid=(pairs,),
        in_specs=[mixed, dy_pair],
        out_specs=pl.BlockSpec((2, rank, rows), lambda p: (p, 0, 0)),
        out_shape=struct((seqs, rank, rows), BF16),
        compiler_params=STEPS,
        name="lower",
    )(got, dy)
    other_low = lax.ppermute(low_g, "c", SWAP)
    part_b = pl.pallas_call(
        functools.partial(tally, scale),
        in_specs=[VMEM],
        out_specs=VMEM,
        out_shape=struct((seqs, tall - rank, width), F32),
        compiler_params=PART,
        name="tally",
    )(got)
    one = pl.BlockSpec((1, rank, rows), lambda s: (s, 0, 0))
    low_g, sent = pl.pallas_call(
        functools.partial(combine, scale),
        grid=(seqs,),
        in_specs=[
            one,
            one,
            pl.BlockSpec((1, tall - rank, width), lambda s: (s, 0, 0)),
            pl.BlockSpec((rows, width), lambda s: (s, 0)),
        ],
        out_specs=(one, pl.BlockSpec((columns, 1, tall, width), lambda s: (0, s, 0, 0))),
        out_shape=(
            struct((seqs, rank, rows), BF16),
            struct((columns, seqs, tall, width), BF16),
        ),
        compiler_params=STEPS,
        name="combine",
    )(low_g, other_low, part_b, activations)
    input_gradient = pl.pallas_call(
        backward,
        grid_spec=pltpu.PrefetchScalarGridSpec(
            num_scalar_prefetch=1,
            grid=(seqs,),
            in_specs=[
                pl.BlockSpec((1, rank, rows), lambda s, slot: (s, 0, 0)),
                pl.BlockSpec((chips, keys, rows), lambda s, slot: (0, 0, s)),
                pl.BlockSpec((chips, keys, rows), lambda s, slot: (0, 0, s)),
                pl.BlockSpec(key_weight.shape, lambda s, slot: (0, 0)),
                pl.BlockSpec((1, 1, tall, width), lambda s, slot: (slot[s] % columns, s, 0, 0)),
            ],
            out_specs=pl.BlockSpec((rows, width), lambda s, slot: (s, 0)),
        ),
        out_shape=struct(activations.shape, BF16),
        compiler_params=ALL,
        cost_estimate=pl.CostEstimate(
            flops=2 * activations.shape[0] * width * (key_weight.shape[1] + rank),
            bytes_accessed=2 * (activations.shape[0] + width) * (key_weight.shape[1] + width),
            transcendentals=0,
        ),
        name="backward",
    )(slot_of, low_g, dy, other_dy, key_weight, panels)
    got = lax.all_to_all(sent, "x", 0, 0, tiled=True)

    sent = pl.pallas_call(
        sort,
        out_shape=struct((slots // columns, tall, width), BF16),
        in_specs=[SMEM, VMEM],
        out_specs=VMEM,
        scratch_shapes=[pltpu.VMEM((slots // columns, tall, width), F32)],
        compiler_params=PART,
        name="sort",
    )(place_of, got)
    got = lax.all_to_all(sent, "z", 0, 0, tiled=True)

    grad_a, grad_b = pl.pallas_call(
        finish,
        out_shape=(struct((1, rank, width), F32), struct((1, rank, keys), F32)),
        in_specs=[VMEM],
        out_specs=(VMEM, VMEM),
        compiler_params=PART,
        name="finish",
    )(got)
    return (input_gradient, grad_a, grad_b)


def solution(mesh):
    columns = min(COLUMNS, mesh.shape["dp"] // 2)
    chips = mesh.shape["mp"] // 2
    grid = Mesh(mesh.devices.reshape(-1, columns, chips, 2), ("z", "x", "y", "c"))
    dp, mp = ("z", "x"), ("y", "c")
    in_specs = (
        P(dp, mp),
        P(dp, mp),
        P(mp, None),
        P(dp, None, mp),
        P(dp, None, mp),
        P(dp),
        P(),
    )
    out_specs = (P(dp, mp), P(dp, None, mp), P(dp, None, mp))
    body = functools.partial(local, columns, chips)
    return jax.shard_map(body, mesh=grid, in_specs=in_specs, out_specs=out_specs, check_vma=False)
```

```python
import functools
import math

import jax
import jax.numpy as jnp
from jax import lax
from jax.experimental import pallas as pl
from jax.experimental.pallas import tpu as pltpu
from jax.sharding import Mesh, PartitionSpec as P

ADAPTER_SCALE = 2.0
F32 = jnp.float32
BF16 = jnp.bfloat16
LANES = 128
COLUMNS = 4
SWAP = [(0, 1), (1, 0)]
WHOLE = pltpu.CompilerParams(vmem_limit_bytes=58 * 2**20)
ALL = pltpu.CompilerParams(vmem_limit_bytes=58 * 2**20, dimension_semantics=("arbitrary",))
STEPS = pltpu.CompilerParams(vmem_limit_bytes=24 * 2**20, dimension_semantics=("arbitrary",))
PART = pltpu.CompilerParams(vmem_limit_bytes=24 * 2**20)
VMEM = pl.BlockSpec(memory_space=pltpu.VMEM)
SMEM = pl.BlockSpec(memory_space=pltpu.SMEM)


def left_half(shape):
    return lax.broadcasted_iota(jnp.int32, shape, 1) < LANES // 2


def pack(tall):
    slabs = []
    for i in range(0, tall.shape[0], 16):
        upper, lower = tall[i : i + 8], pltpu.roll(tall[i + 8 : i + 16], LANES // 2, 1)
        slabs.append(jnp.where(left_half(upper.shape), upper, lower))
    return jnp.concatenate(slabs, axis=1)


def unpack(flat, right):
    pieces = []
    for i in range(0, flat.shape[1], LANES):
        slab = flat[:, i : i + LANES]
        turned = pltpu.roll(slab, LANES // 2, 1)
        left = left_half(slab.shape)
        for piece in (turned, slab) if right else (slab, turned):
            pieces.append(jnp.where(left != right, piece, 0.0))
    return jnp.concatenate(pieces, axis=0)


def prepare(down_ref, up_ref, sent_ref):
    up = up_ref[0].astype(F32).T
    packed = pack(jnp.concatenate([up, jnp.zeros_like(up)], axis=1))
    panel = jnp.concatenate([down_ref[0].astype(F32), packed], axis=0).astype(BF16)
    for z in range(sent_ref.shape[0]):
        sent_ref[z] = panel


def select(columns, panel_ref, holder_ref, *refs):
    tenant_refs, (sent_ref, slot_ref, place_ref, table) = refs[:columns], refs[-4:]
    seqs = sent_ref.shape[1]
    for t in range(holder_ref.shape[0]):
        table[holder_ref[t]] = jnp.int32(t)
    here = lax.axis_index("x")
    for back, tenant_ref in enumerate(tenant_refs):
        there = lax.rem(here + columns - back, columns)
        for s in range(seqs):
            slot = table[tenant_ref[s]]
            row, column = slot // columns, slot % columns
            if back == 0:
                slot_ref[s] = slot
            place_ref[there * seqs + s] = jnp.where(column == here, row, -1)
            sent_ref[there, s] = panel_ref[row]


def bring(x_ref, *refs):
    out_ref, sem = refs[-2:]
    copy = pltpu.make_async_copy(x_ref, out_ref, sem)
    copy.start()
    copy.wait()


def bring_half(dy_ref, *refs):
    out_ref, sem = refs[-2:]
    core = lax.axis_index("c")
    copies = [
        pltpu.make_async_copy(dy_ref.at[y, core], out_ref.at[y], sem.at[y])
        for y in range(out_ref.shape[0])
    ]
    for copy in copies:
        copy.start()
    for copy in copies:
        copy.wait()


def low(slot_ref, panel0_ref, panel1_ref, x_ref, low_ref, down_ref, ups_ref):
    rows, rank = low_ref.shape[1], low_ref.shape[2] // 2
    total = ups = 0.0
    for side, panel_ref in enumerate((panel0_ref, panel1_ref)):
        panel = panel_ref[0, 0]
        down = panel[:rank]
        down_ref[side] = down
        blank = jnp.zeros_like(down)
        wide = jnp.concatenate([blank, down] if side else [down, blank], axis=0)
        total = total + lax.dot_general(
            x_ref[side * rows : (side + 1) * rows],
            wide,
            (((1,), (1,)), ((), ())),
            preferred_element_type=F32,
        )
        ups = ups + unpack(panel.astype(F32)[rank:], side == 1)
    low_ref[0] = total.astype(BF16)
    ups_ref[0] = ups.astype(BF16)


def project(low_ref, other_ref, ups_ref, dy_ref, sent_ref):
    rows = low_ref.shape[1]
    chips, keys, _ = dy_ref.shape
    low_u = (low_ref[0].astype(F32) + other_ref[0].astype(F32)).astype(BF16)
    dy = dy_ref[...].reshape(chips * keys, 2 * rows)
    parts = [
        jnp.dot(dy[:, side * rows : (side + 1) * rows], low_u, preferred_element_type=F32)
        for side in range(2)
    ]
    part = jnp.where(left_half(parts[0].shape), parts[0], parts[1])
    sent_ref[:, 0, :keys] = part.reshape(chips, keys, LANES).astype(BF16)
    for y in range(chips):
        sent_ref[y, 0, keys:] = ups_ref[0]


def lower(got_ref, dy_ref, low_ref):
    _, rank, rows = low_ref.shape
    chips, keys, _ = dy_ref.shape
    ups = got_ref[:, 0, keys:].reshape(chips * keys, LANES)
    dy = dy_ref[...].reshape(chips * keys, 2 * rows)
    for side in range(2):
        both = lax.dot_general(
            ups,
            dy[:, side * rows : (side + 1) * rows],
            (((0,), (0,)), ((), ())),
            preferred_element_type=F32,
        )
        low_ref[side] = both[side * rank : (side + 1) * rank].astype(BF16)


def tally(scale, got_ref, part_ref):
    keys = got_ref.shape[2] // 2
    for pair in range(got_ref.shape[1]):
        total = 0.0
        for y in range(got_ref.shape[0]):
            total = total + got_ref[y, pair, :keys].astype(F32)
        total = scale * total
        part_ref[2 * pair] = pack(total)
        part_ref[2 * pair + 1] = pack(pltpu.roll(total, LANES // 2, 1))


def combine(scale, low_ref, other_ref, part_ref, x_ref, low_g_ref, sent_ref):
    low_g = (low_ref[0].astype(F32) + other_ref[0].astype(F32)).astype(BF16)
    low_g_ref[0] = low_g
    part_a = scale * jnp.dot(low_g, x_ref[...], preferred_element_type=F32)
    panel = jnp.concatenate([part_a, part_ref[0]], axis=0).astype(BF16)
    for x in range(sent_ref.shape[0]):
        sent_ref[x, 0] = panel


def backward(low_ref, dy_ref, weight_ref, down_ref, input_ref):
    frozen = lax.dot_general(
        dy_ref[...], weight_ref[...], (((0,), (1,)), ((), ())), preferred_element_type=F32
    )
    update = lax.dot_general(
        low_ref[0], down_ref[0], (((0,), (0,)), ((), ())), preferred_element_type=F32
    )
    input_ref[...] = (frozen + ADAPTER_SCALE * update).astype(BF16)


def sort(place_ref, got_ref, sent_ref, total):
    columns, seqs = got_ref.shape[:2]
    total[...] = jnp.zeros_like(total)
    for x in range(columns):
        for s in range(seqs):
            place = place_ref[x * seqs + s]

            @pl.when(place >= 0)
            def _():
                total[place] += got_ref[x, s].astype(F32)

    sent_ref[...] = total[...].astype(BF16)


def finish(got_ref, down_ref, up_ref):
    rank = down_ref.shape[1]
    total = got_ref[0].astype(F32)
    for p in range(1, got_ref.shape[0]):
        total = total + got_ref[p].astype(F32)
    down_ref[0] = total[:rank]
    up_ref[0] = unpack(total[rank:], False)[:, :rank].T


def local(
    columns,
    chips,
    activations,
    cotangent,
    key_weight,
    adapter_down,
    adapter_up,
    sequence_tenant,
    slot_holder_tenant,
):
    seqs = sequence_tenant.shape[0]
    rows = activations.shape[0] // seqs
    width = activations.shape[1]
    keys = cotangent.shape[1]
    rank = adapter_down.shape[1]
    slots = slot_holder_tenant.shape[0]
    tall = rank + rank * keys // width
    scale = ADAPTER_SCALE / math.sqrt(seqs * rows)
    struct = jax.ShapeDtypeStruct

    dy = lax.all_gather(cotangent.T, ("y", "c"), axis=0, tiled=True)
    dy_halves = dy.reshape(chips, 2, keys, dy.shape[1])

    anywhere = pl.BlockSpec(memory_space=pl.ANY)
    near_x = pl.pallas_call(
        bring,
        out_shape=struct(activations.shape, BF16),
        in_specs=[anywhere],
        out_specs=anywhere,
        scratch_shapes=[pltpu.SemaphoreType.DMA],
        compiler_params=PART,
        name="bring_x",
    )(activations)

    tenants = [sequence_tenant] + [
        lax.ppermute(sequence_tenant, "x", [(x, (x + d) % columns) for x in range(columns)])
        for d in range(1, columns)
    ]
    sent = pl.pallas_call(
        prepare,
        out_shape=struct((slots // columns, tall, width), BF16),
        in_specs=[VMEM, VMEM],
        out_specs=VMEM,
        compiler_params=WHOLE,
        name="prepare",
    )(adapter_down, adapter_up)
    panels = lax.all_to_all(sent, "z", 0, 0, tiled=True)
    sent, slot_of, place_of = pl.pallas_call(
        functools.partial(select, columns),
        out_shape=(
            struct((columns, seqs, tall, width), BF16),
            struct((seqs,), jnp.int32),
            struct((columns * seqs,), jnp.int32),
        ),
        in_specs=[VMEM] + [SMEM] * (1 + columns) + [anywhere],
        out_specs=(VMEM, SMEM, SMEM),
        scratch_shapes=[pltpu.SMEM((slots,), jnp.int32)],
        compiler_params=PART,
        name="select",
    )(panels, slot_holder_tenant, *tenants, near_x)
    panels = lax.all_to_all(sent, "x", 0, 0, tiled=True)

    pairs = seqs // 2
    low_u, down, ups = pl.pallas_call(
        low,
        grid_spec=pltpu.PrefetchScalarGridSpec(
            num_scalar_prefetch=1,
            grid=(pairs,),
            in_specs=[
                pl.BlockSpec(
                    (1, 1, tall, width),
                    lambda p, slot: (slot[2 * p] % columns, 2 * p, 0, 0),
                ),
                pl.BlockSpec(
                    (1, 1, tall, width),
                    lambda p, slot: (slot[2 * p + 1] % columns, 2 * p + 1, 0, 0),
                ),
                pl.BlockSpec((2 * rows, width), lambda p, slot: (p, 0)),
            ],
            out_specs=(
                pl.BlockSpec((1, rows, 2 * rank), lambda p, slot: (p, 0, 0)),
                pl.BlockSpec((2, rank, width), lambda p, slot: (p, 0, 0)),
                pl.BlockSpec((1, keys, 2 * rank), lambda p, slot: (p, 0, 0)),
            ),
        ),
        out_shape=(
            struct((pairs, rows, 2 * rank), BF16),
            struct((seqs, rank, width), BF16),
            struct((pairs, keys, 2 * rank), BF16),
        ),
        compiler_params=STEPS,
        name="low",
    )(slot_of, panels, panels, near_x)
    other_low = lax.ppermute(low_u, "c", SWAP)
    half_dy = pl.pallas_call(
        bring_half,
        out_shape=struct((chips, keys, dy.shape[1]), BF16),
        in_specs=[anywhere, anywhere],
        out_specs=anywhere,
        scratch_shapes=[pltpu.SemaphoreType.DMA((chips,))],
        compiler_params=PART,
        name="bring_dy",
    )(dy_halves, low_u)
    dy_pair = pl.BlockSpec((chips, keys, 2 * rows), lambda p: (0, 0, p))
    mixed = pl.BlockSpec((chips, 1, 2 * keys, 2 * rank), lambda p: (0, p, 0, 0))
    sent = pl.pallas_call(
        project,
        grid=(pairs,),
        in_specs=[
            pl.BlockSpec((1, rows, 2 * rank), lambda p: (p, 0, 0)),
            pl.BlockSpec((1, rows, 2 * rank), lambda p: (p, 0, 0)),
            pl.BlockSpec((1, keys, 2 * rank), lambda p: (p, 0, 0)),
            dy_pair,
        ],
        out_specs=mixed,
        out_shape=struct((chips, pairs, 2 * keys, 2 * rank), BF16),
        compiler_params=STEPS,
        name="project",
    )(low_u, other_low, ups, half_dy)
    got = lax.all_to_all(sent, "y", 0, 0, tiled=True)

    low_g = pl.pallas_call(
        lower,
        grid=(pairs,),
        in_specs=[mixed, dy_pair],
        out_specs=pl.BlockSpec((2, rank, rows), lambda p: (p, 0, 0)),
        out_shape=struct((seqs, rank, rows), BF16),
        compiler_params=STEPS,
        name="lower",
    )(got, half_dy)
    other_low = lax.ppermute(low_g, "c", SWAP)
    part_b = pl.pallas_call(
        functools.partial(tally, scale),
        in_specs=[VMEM],
        out_specs=VMEM,
        out_shape=struct((seqs, tall - rank, width), F32),
        compiler_params=PART,
        name="tally",
    )(got)
    one = pl.BlockSpec((1, rank, rows), lambda s: (s, 0, 0))
    low_g, sent = pl.pallas_call(
        functools.partial(combine, scale),
        grid=(seqs,),
        in_specs=[
            one,
            one,
            pl.BlockSpec((1, tall - rank, width), lambda s: (s, 0, 0)),
            pl.BlockSpec((rows, width), lambda s: (s, 0)),
        ],
        out_specs=(one, pl.BlockSpec((columns, 1, tall, width), lambda s: (0, s, 0, 0))),
        out_shape=(
            struct((seqs, rank, rows), BF16),
            struct((columns, seqs, tall, width), BF16),
        ),
        compiler_params=STEPS,
        name="combine",
    )(low_g, other_low, part_b, near_x)
    input_gradient = pl.pallas_call(
        backward,
        grid=(seqs,),
        in_specs=[
            one,
            pl.BlockSpec((dy.shape[0], rows), lambda s: (0, s)),
            pl.BlockSpec(key_weight.shape, lambda s: (0, 0)),
            pl.BlockSpec((1, rank, width), lambda s: (s, 0, 0)),
        ],
        out_specs=pl.BlockSpec((rows, width), lambda s: (s, 0)),
        out_shape=struct(activations.shape, BF16),
        compiler_params=ALL,
        cost_estimate=pl.CostEstimate(
            flops=2 * activations.shape[0] * width * (key_weight.shape[1] + rank),
            bytes_accessed=2 * (activations.shape[0] + width) * (key_weight.shape[1] + width),
            transcendentals=0,
        ),
        name="backward",
    )(low_g, dy, key_weight, down)
    got = lax.all_to_all(sent, "x", 0, 0, tiled=True)

    sent = pl.pallas_call(
        sort,
        out_shape=struct((slots // columns, tall, width), BF16),
        in_specs=[SMEM, VMEM],
        out_specs=VMEM,
        scratch_shapes=[pltpu.VMEM((slots // columns, tall, width), F32)],
        compiler_params=PART,
        name="sort",
    )(place_of, got)
    got = lax.all_to_all(sent, "z", 0, 0, tiled=True)

    grad_a, grad_b = pl.pallas_call(
        finish,
        out_shape=(struct((1, rank, width), F32), struct((1, rank, keys), F32)),
        in_specs=[VMEM],
        out_specs=(VMEM, VMEM),
        compiler_params=PART,
        name="finish",
    )(got)
    return (input_gradient, grad_a, grad_b)


def solution(mesh):
    columns = min(COLUMNS, mesh.shape["dp"] // 2)
    chips = mesh.shape["mp"] // 2
    grid = Mesh(mesh.devices.reshape(-1, columns, chips, 2), ("z", "x", "y", "c"))
    dp, mp = ("z", "x"), ("y", "c")
    in_specs = (
        P(dp, mp),
        P(dp, mp),
        P(mp, None),
        P(dp, None, mp),
        P(dp, None, mp),
        P(dp),
        P(),
    )
    out_specs = (P(dp, mp), P(dp, None, mp), P(dp, None, mp))
    body = functools.partial(local, columns, chips)
    return jax.shard_map(body, mesh=grid, in_specs=in_specs, out_specs=out_specs, check_vma=False)
```

```python
import functools
import math

import jax
import jax.numpy as jnp
from jax import lax
from jax.experimental import pallas as pl
from jax.experimental.pallas import tpu as pltpu
from jax.sharding import Mesh, PartitionSpec as P

ADAPTER_SCALE = 2.0
F32 = jnp.float32
BF16 = jnp.bfloat16
LANES = 128
COLUMNS = 4
SWAP = [(0, 1), (1, 0)]
WHOLE = pltpu.CompilerParams(vmem_limit_bytes=58 * 2**20)
ALL = pltpu.CompilerParams(vmem_limit_bytes=58 * 2**20, dimension_semantics=("arbitrary",))
STEPS = pltpu.CompilerParams(vmem_limit_bytes=24 * 2**20, dimension_semantics=("arbitrary",))
PART = pltpu.CompilerParams(vmem_limit_bytes=24 * 2**20)
VMEM = pl.BlockSpec(memory_space=pltpu.VMEM)
SMEM = pl.BlockSpec(memory_space=pltpu.SMEM)


def left_half(shape):
    return lax.broadcasted_iota(jnp.int32, shape, 1) < LANES // 2


def pack(tall):
    slabs = []
    for i in range(0, tall.shape[0], 16):
        upper, lower = tall[i : i + 8], pltpu.roll(tall[i + 8 : i + 16], LANES // 2, 1)
        slabs.append(jnp.where(left_half(upper.shape), upper, lower))
    return jnp.concatenate(slabs, axis=1)


def unpack(flat, right):
    pieces = []
    for i in range(0, flat.shape[1], LANES):
        slab = flat[:, i : i + LANES]
        turned = pltpu.roll(slab, LANES // 2, 1)
        left = left_half(slab.shape)
        for piece in (turned, slab) if right else (slab, turned):
            pieces.append(jnp.where(left != right, piece, 0.0))
    return jnp.concatenate(pieces, axis=0)


def prepare(down_ref, up_ref, sent_ref):
    up = up_ref[0].astype(F32).T
    packed = pack(jnp.concatenate([up, jnp.zeros_like(up)], axis=1))
    panel = jnp.concatenate([down_ref[0].astype(F32), packed], axis=0).astype(BF16)
    for z in range(sent_ref.shape[0]):
        sent_ref[z] = panel


def select(columns, panel_ref, holder_ref, *refs):
    tenant_refs, (sent_ref, slot_ref, place_ref, table) = refs[:columns], refs[-4:]
    seqs = sent_ref.shape[1]
    for t in range(holder_ref.shape[0]):
        table[holder_ref[t]] = jnp.int32(t)
    here = lax.axis_index("x")
    slot_ref[seqs] = lax.axis_index("c")
    for back, tenant_ref in enumerate(tenant_refs):
        there = lax.rem(here + columns - back, columns)
        for s in range(seqs):
            slot = table[tenant_ref[s]]
            row, column = slot // columns, slot % columns
            if back == 0:
                slot_ref[s] = slot
            place_ref[there * seqs + s] = jnp.where(column == here, row, -1)
            sent_ref[there, s] = panel_ref[row]


def bring(x_ref, *refs):
    out_ref, sem = refs[-2:]
    copy = pltpu.make_async_copy(x_ref, out_ref, sem)
    copy.start()
    copy.wait()


def low(slot_ref, panel0_ref, panel1_ref, x_ref, low_ref, down_ref, ups_ref):
    rows, rank = low_ref.shape[1], low_ref.shape[2] // 2
    total = ups = 0.0
    for side, panel_ref in enumerate((panel0_ref, panel1_ref)):
        panel = panel_ref[0, 0]
        down = panel[:rank]
        down_ref[side] = down
        blank = jnp.zeros_like(down)
        wide = jnp.concatenate([blank, down] if side else [down, blank], axis=0)
        total = total + lax.dot_general(
            x_ref[side * rows : (side + 1) * rows],
            wide,
            (((1,), (1,)), ((), ())),
            preferred_element_type=F32,
        )
        ups = ups + unpack(panel.astype(F32)[rank:], side == 1)
    low_ref[0] = total.astype(BF16)
    ups_ref[0] = ups.astype(BF16)


def project(slot_ref, low_ref, other_ref, ups_ref, dy_ref, sent_ref):
    rows = low_ref.shape[1]
    chips, _, keys, _ = dy_ref.shape
    low_u = (low_ref[0].astype(F32) + other_ref[0].astype(F32)).astype(BF16)
    dy = dy_ref[...].reshape(chips * keys, 2 * rows)
    parts = [
        jnp.dot(dy[:, side * rows : (side + 1) * rows], low_u, preferred_element_type=F32)
        for side in range(2)
    ]
    part = jnp.where(left_half(parts[0].shape), parts[0], parts[1])
    sent_ref[:, 0, :keys] = part.reshape(chips, keys, LANES).astype(BF16)
    for y in range(chips):
        sent_ref[y, 0, keys:] = ups_ref[0]


def lower(slot_ref, got_ref, dy_ref, low_ref):
    _, rank, rows = low_ref.shape
    chips, _, keys, _ = dy_ref.shape
    ups = got_ref[:, 0, keys:].reshape(chips * keys, LANES)
    dy = dy_ref[...].reshape(chips * keys, 2 * rows)
    for side in range(2):
        both = lax.dot_general(
            ups,
            dy[:, side * rows : (side + 1) * rows],
            (((0,), (0,)), ((), ())),
            preferred_element_type=F32,
        )
        low_ref[side] = both[side * rank : (side + 1) * rank].astype(BF16)


def tally(scale, got_ref, part_ref):
    keys = got_ref.shape[2] // 2
    for pair in range(got_ref.shape[1]):
        total = 0.0
        for y in range(got_ref.shape[0]):
            total = total + got_ref[y, pair, :keys].astype(F32)
        total = scale * total
        part_ref[2 * pair] = pack(total)
        part_ref[2 * pair + 1] = pack(pltpu.roll(total, LANES // 2, 1))


def combine(scale, low_ref, other_ref, part_ref, x_ref, low_g_ref, sent_ref):
    low_g = (low_ref[0].astype(F32) + other_ref[0].astype(F32)).astype(BF16)
    low_g_ref[0] = low_g
    part_a = scale * jnp.dot(low_g, x_ref[...], preferred_element_type=F32)
    panel = jnp.concatenate([part_a, part_ref[0]], axis=0).astype(BF16)
    for x in range(sent_ref.shape[0]):
        sent_ref[x, 0] = panel


def backward(low_ref, dy_ref, weight_ref, down_ref, input_ref):
    frozen = lax.dot_general(
        dy_ref[...], weight_ref[...], (((0,), (1,)), ((), ())), preferred_element_type=F32
    )
    update = lax.dot_general(
        low_ref[0], down_ref[0], (((0,), (0,)), ((), ())), preferred_element_type=F32
    )
    input_ref[...] = (frozen + ADAPTER_SCALE * update).astype(BF16)


def sort(place_ref, got_ref, sent_ref, total):
    columns, seqs = got_ref.shape[:2]
    total[...] = jnp.zeros_like(total)
    for x in range(columns):
        for s in range(seqs):
            place = place_ref[x * seqs + s]

            @pl.when(place >= 0)
            def _():
                total[place] += got_ref[x, s].astype(F32)

    sent_ref[...] = total[...].astype(BF16)


def finish(got_ref, down_ref, up_ref):
    rank = down_ref.shape[1]
    total = got_ref[0].astype(F32)
    for p in range(1, got_ref.shape[0]):
        total = total + got_ref[p].astype(F32)
    down_ref[0] = total[:rank]
    up_ref[0] = unpack(total[rank:], False)[:, :rank].T


def local(
    columns,
    chips,
    activations,
    cotangent,
    key_weight,
    adapter_down,
    adapter_up,
    sequence_tenant,
    slot_holder_tenant,
):
    seqs = sequence_tenant.shape[0]
    rows = activations.shape[0] // seqs
    width = activations.shape[1]
    keys = cotangent.shape[1]
    rank = adapter_down.shape[1]
    slots = slot_holder_tenant.shape[0]
    tall = rank + rank * keys // width
    scale = ADAPTER_SCALE / math.sqrt(seqs * rows)
    struct = jax.ShapeDtypeStruct

    dy = lax.all_gather(cotangent.T, ("y", "c"), axis=0, tiled=True)

    anywhere = pl.BlockSpec(memory_space=pl.ANY)
    near_x = pl.pallas_call(
        bring,
        out_shape=struct(activations.shape, BF16),
        in_specs=[anywhere],
        out_specs=anywhere,
        scratch_shapes=[pltpu.SemaphoreType.DMA],
        compiler_params=PART,
        name="bring_x",
    )(activations)

    tenants = [sequence_tenant] + [
        lax.ppermute(sequence_tenant, "x", [(x, (x + d) % columns) for x in range(columns)])
        for d in range(1, columns)
    ]
    sent = pl.pallas_call(
        prepare,
        out_shape=struct((slots // columns, tall, width), BF16),
        in_specs=[VMEM, VMEM],
        out_specs=VMEM,
        compiler_params=WHOLE,
        name="prepare",
    )(adapter_down, adapter_up)
    panels = lax.all_to_all(sent, "z", 0, 0, tiled=True)
    sent, slot_of, place_of = pl.pallas_call(
        functools.partial(select, columns),
        out_shape=(
            struct((columns, seqs, tall, width), BF16),
            struct((seqs + 1,), jnp.int32),
            struct((columns * seqs,), jnp.int32),
        ),
        in_specs=[VMEM] + [SMEM] * (1 + columns) + [anywhere],
        out_specs=(VMEM, SMEM, SMEM),
        scratch_shapes=[pltpu.SMEM((slots,), jnp.int32)],
        compiler_params=PART,
        name="select",
    )(panels, slot_holder_tenant, *tenants, near_x)
    panels = lax.all_to_all(sent, "x", 0, 0, tiled=True)
    panels, dy = lax.optimization_barrier((panels, dy))
    dy_halves = dy.reshape(chips, 2, keys, dy.shape[1])

    pairs = seqs // 2
    low_u, down, ups = pl.pallas_call(
        low,
        grid_spec=pltpu.PrefetchScalarGridSpec(
            num_scalar_prefetch=1,
            grid=(pairs,),
            in_specs=[
                pl.BlockSpec(
                    (1, 1, tall, width),
                    lambda p, slot: (slot[2 * p] % columns, 2 * p, 0, 0),
                ),
                pl.BlockSpec(
                    (1, 1, tall, width),
                    lambda p, slot: (slot[2 * p + 1] % columns, 2 * p + 1, 0, 0),
                ),
                pl.BlockSpec((2 * rows, width), lambda p, slot: (p, 0)),
            ],
            out_specs=(
                pl.BlockSpec((1, rows, 2 * rank), lambda p, slot: (p, 0, 0)),
                pl.BlockSpec((2, rank, width), lambda p, slot: (p, 0, 0)),
                pl.BlockSpec((1, keys, 2 * rank), lambda p, slot: (p, 0, 0)),
            ),
        ),
        out_shape=(
            struct((pairs, rows, 2 * rank), BF16),
            struct((seqs, rank, width), BF16),
            struct((pairs, keys, 2 * rank), BF16),
        ),
        compiler_params=STEPS,
        name="low",
    )(slot_of, panels, panels, near_x)
    other_low = lax.ppermute(low_u, "c", SWAP)
    dy_pair = pl.BlockSpec(
        (chips, 1, keys, 2 * rows), lambda p, slot: (0, slot[seqs], 0, p)
    )
    mixed = pl.BlockSpec((chips, 1, 2 * keys, 2 * rank), lambda p, slot: (0, p, 0, 0))
    sent = pl.pallas_call(
        project,
        grid_spec=pltpu.PrefetchScalarGridSpec(
            num_scalar_prefetch=1,
            grid=(pairs,),
            in_specs=[
                pl.BlockSpec((1, rows, 2 * rank), lambda p, slot: (p, 0, 0)),
                pl.BlockSpec((1, rows, 2 * rank), lambda p, slot: (p, 0, 0)),
                pl.BlockSpec((1, keys, 2 * rank), lambda p, slot: (p, 0, 0)),
                dy_pair,
            ],
            out_specs=mixed,
        ),
        out_shape=struct((chips, pairs, 2 * keys, 2 * rank), BF16),
        compiler_params=STEPS,
        name="project",
    )(slot_of, low_u, other_low, ups, dy_halves)
    got = lax.all_to_all(sent, "y", 0, 0, tiled=True)

    low_g = pl.pallas_call(
        lower,
        grid_spec=pltpu.PrefetchScalarGridSpec(
            num_scalar_prefetch=1,
            grid=(pairs,),
            in_specs=[mixed, dy_pair],
            out_specs=pl.BlockSpec((2, rank, rows), lambda p, slot: (p, 0, 0)),
        ),
        out_shape=struct((seqs, rank, rows), BF16),
        compiler_params=STEPS,
        name="lower",
    )(slot_of, got, dy_halves)
    other_low = lax.ppermute(low_g, "c", SWAP)
    part_b = pl.pallas_call(
        functools.partial(tally, scale),
        in_specs=[VMEM],
        out_specs=VMEM,
        out_shape=struct((seqs, tall - rank, width), F32),
        compiler_params=PART,
        name="tally",
    )(got)
    one = pl.BlockSpec((1, rank, rows), lambda s: (s, 0, 0))
    low_g, sent = pl.pallas_call(
        functools.partial(combine, scale),
        grid=(seqs,),
        in_specs=[
            one,
            one,
            pl.BlockSpec((1, tall - rank, width), lambda s: (s, 0, 0)),
            pl.BlockSpec((rows, width), lambda s: (s, 0)),
        ],
        out_specs=(one, pl.BlockSpec((columns, 1, tall, width), lambda s: (0, s, 0, 0))),
        out_shape=(
            struct((seqs, rank, rows), BF16),
            struct((columns, seqs, tall, width), BF16),
        ),
        compiler_params=STEPS,
        name="combine",
    )(low_g, other_low, part_b, near_x)
    input_gradient = pl.pallas_call(
        backward,
        grid=(seqs,),
        in_specs=[
            one,
            pl.BlockSpec((dy.shape[0], rows), lambda s: (0, s)),
            pl.BlockSpec(key_weight.shape, lambda s: (0, 0)),
            pl.BlockSpec((1, rank, width), lambda s: (s, 0, 0)),
        ],
        out_specs=pl.BlockSpec((rows, width), lambda s: (s, 0)),
        out_shape=struct(activations.shape, BF16),
        compiler_params=ALL,
        cost_estimate=pl.CostEstimate(
            flops=2 * activations.shape[0] * width * (key_weight.shape[1] + rank),
            bytes_accessed=2 * (activations.shape[0] + width) * (key_weight.shape[1] + width),
            transcendentals=0,
        ),
        name="backward",
    )(low_g, dy, key_weight, down)
    got = lax.all_to_all(sent, "x", 0, 0, tiled=True)

    sent = pl.pallas_call(
        sort,
        out_shape=struct((slots // columns, tall, width), BF16),
        in_specs=[SMEM, VMEM],
        out_specs=VMEM,
        scratch_shapes=[pltpu.VMEM((slots // columns, tall, width), F32)],
        compiler_params=PART,
        name="sort",
    )(place_of, got)
    got = lax.all_to_all(sent, "z", 0, 0, tiled=True)

    grad_a, grad_b = pl.pallas_call(
        finish,
        out_shape=(struct((1, rank, width), F32), struct((1, rank, keys), F32)),
        in_specs=[VMEM],
        out_specs=(VMEM, VMEM),
        compiler_params=PART,
        name="finish",
    )(got)
    return (input_gradient, grad_a, grad_b)


def solution(mesh):
    columns = min(COLUMNS, mesh.shape["dp"] // 2)
    chips = mesh.shape["mp"] // 2
    grid = Mesh(mesh.devices.reshape(-1, columns, chips, 2), ("z", "x", "y", "c"))
    dp, mp = ("z", "x"), ("y", "c")
    in_specs = (
        P(dp, mp),
        P(dp, mp),
        P(mp, None),
        P(dp, None, mp),
        P(dp, None, mp),
        P(dp),
        P(),
    )
    out_specs = (P(dp, mp), P(dp, None, mp), P(dp, None, mp))
    body = functools.partial(local, columns, chips)
    return jax.shard_map(body, mesh=grid, in_specs=in_specs, out_specs=out_specs, check_vma=False)
```

```python
import functools
import math

import jax
import jax.numpy as jnp
from jax import lax
from jax.experimental import pallas as pl
from jax.experimental.pallas import tpu as pltpu
from jax.sharding import Mesh, PartitionSpec as P

ADAPTER_SCALE = 2.0
F32 = jnp.float32
BF16 = jnp.bfloat16
LANES = 128
COLUMNS = 4
SWAP = [(0, 1), (1, 0)]
WHOLE = pltpu.CompilerParams(vmem_limit_bytes=58 * 2**20)
ALL = pltpu.CompilerParams(vmem_limit_bytes=58 * 2**20, dimension_semantics=("arbitrary",))
STEPS = pltpu.CompilerParams(vmem_limit_bytes=24 * 2**20, dimension_semantics=("arbitrary",))
PART = pltpu.CompilerParams(vmem_limit_bytes=24 * 2**20)
VMEM = pl.BlockSpec(memory_space=pltpu.VMEM)
SMEM = pl.BlockSpec(memory_space=pltpu.SMEM)


def left_half(shape):
    return lax.broadcasted_iota(jnp.int32, shape, 1) < LANES // 2


def pack(tall):
    slabs = []
    for i in range(0, tall.shape[0], 16):
        upper, lower = tall[i : i + 8], pltpu.roll(tall[i + 8 : i + 16], LANES // 2, 1)
        slabs.append(jnp.where(left_half(upper.shape), upper, lower))
    return jnp.concatenate(slabs, axis=1)


def unpack(flat, right):
    pieces = []
    for i in range(0, flat.shape[1], LANES):
        slab = flat[:, i : i + LANES]
        turned = pltpu.roll(slab, LANES // 2, 1)
        left = left_half(slab.shape)
        for piece in (turned, slab) if right else (slab, turned):
            pieces.append(jnp.where(left != right, piece, 0.0))
    return jnp.concatenate(pieces, axis=0)


def prepare(down_ref, up_ref, sent_ref):
    up = up_ref[0].astype(F32).T
    packed = pack(jnp.concatenate([up, jnp.zeros_like(up)], axis=1))
    panel = jnp.concatenate([down_ref[0].astype(F32), packed], axis=0).astype(BF16)
    for z in range(sent_ref.shape[0]):
        sent_ref[z] = panel


def select(columns, panel_ref, holder_ref, *refs):
    tenant_refs, (sent_ref, slot_ref, place_ref, table) = refs[:columns], refs[-4:]
    seqs = sent_ref.shape[1]
    for t in range(holder_ref.shape[0]):
        table[holder_ref[t]] = jnp.int32(t)
    here = lax.axis_index("x")
    slot_ref[seqs] = lax.axis_index("c")
    for back, tenant_ref in enumerate(tenant_refs):
        there = lax.rem(here + columns - back, columns)
        for s in range(seqs):
            slot = table[tenant_ref[s]]
            row, column = slot // columns, slot % columns
            if back == 0:
                slot_ref[s] = slot
            place_ref[there * seqs + s] = jnp.where(column == here, row, -1)
            sent_ref[there, s] = panel_ref[row]


def bring(x_ref, *refs):
    out_ref, sem = refs[-2:]
    copy = pltpu.make_async_copy(x_ref, out_ref, sem)
    copy.start()
    copy.wait()


def low(slot_ref, panel0_ref, panel1_ref, x_ref, low_ref, ups_ref):
    rows, rank = low_ref.shape[1], low_ref.shape[2] // 2
    total = ups = 0.0
    for side, panel_ref in enumerate((panel0_ref, panel1_ref)):
        panel = panel_ref[0, 0]
        down = panel[:rank]
        blank = jnp.zeros_like(down)
        wide = jnp.concatenate([blank, down] if side else [down, blank], axis=0)
        total = total + lax.dot_general(
            x_ref[side * rows : (side + 1) * rows],
            wide,
            (((1,), (1,)), ((), ())),
            preferred_element_type=F32,
        )
        ups = ups + unpack(panel.astype(F32)[rank:], side == 1)
    low_ref[0] = total.astype(BF16)
    ups_ref[0] = ups.astype(BF16)


def keep(slot_ref, panel_ref, _, down_ref):
    seqs, rank, _ = down_ref.shape
    for s in range(seqs):
        down_ref[s] = panel_ref[lax.rem(slot_ref[s], panel_ref.shape[0]), s][:rank]


def project(slot_ref, low_ref, other_ref, ups_ref, dy_ref, sent_ref):
    rows = low_ref.shape[1]
    chips, _, keys, _ = dy_ref.shape
    low_u = (low_ref[0].astype(F32) + other_ref[0].astype(F32)).astype(BF16)
    dy = dy_ref[...].reshape(chips * keys, 2 * rows)
    parts = [
        jnp.dot(dy[:, side * rows : (side + 1) * rows], low_u, preferred_element_type=F32)
        for side in range(2)
    ]
    part = jnp.where(left_half(parts[0].shape), parts[0], parts[1])
    sent_ref[:, 0, :keys] = part.reshape(chips, keys, LANES).astype(BF16)
    for y in range(chips):
        sent_ref[y, 0, keys:] = ups_ref[0]


def lower(slot_ref, got_ref, dy_ref, low_ref):
    _, rank, rows = low_ref.shape
    chips, _, keys, _ = dy_ref.shape
    ups = got_ref[:, 0, keys:].reshape(chips * keys, LANES)
    dy = dy_ref[...].reshape(chips * keys, 2 * rows)
    for side in range(2):
        both = lax.dot_general(
            ups,
            dy[:, side * rows : (side + 1) * rows],
            (((0,), (0,)), ((), ())),
            preferred_element_type=F32,
        )
        low_ref[side] = both[side * rank : (side + 1) * rank].astype(BF16)


def tally(scale, got_ref, part_ref):
    keys = got_ref.shape[2] // 2
    for pair in range(got_ref.shape[1]):
        total = 0.0
        for y in range(got_ref.shape[0]):
            total = total + got_ref[y, pair, :keys].astype(F32)
        total = scale * total
        part_ref[2 * pair] = pack(total)
        part_ref[2 * pair + 1] = pack(pltpu.roll(total, LANES // 2, 1))


def combine(scale, low_ref, other_ref, part_ref, x_ref, low_g_ref, sent_ref):
    low_g = (low_ref[0].astype(F32) + other_ref[0].astype(F32)).astype(BF16)
    low_g_ref[0] = low_g
    part_a = scale * jnp.dot(low_g, x_ref[...], preferred_element_type=F32)
    panel = jnp.concatenate([part_a, part_ref[0]], axis=0).astype(BF16)
    for x in range(sent_ref.shape[0]):
        sent_ref[x, 0] = panel


def backward(low_ref, dy_ref, weight_ref, down_ref, input_ref):
    frozen = lax.dot_general(
        dy_ref[...], weight_ref[...], (((0,), (1,)), ((), ())), preferred_element_type=F32
    )
    update = lax.dot_general(
        low_ref[0], down_ref[0], (((0,), (0,)), ((), ())), preferred_element_type=F32
    )
    input_ref[...] = (frozen + ADAPTER_SCALE * update).astype(BF16)


def sort(place_ref, got_ref, sent_ref, total):
    columns, seqs = got_ref.shape[:2]
    total[...] = jnp.zeros_like(total)
    for x in range(columns):
        for s in range(seqs):
            place = place_ref[x * seqs + s]

            @pl.when(place >= 0)
            def _():
                total[place] += got_ref[x, s].astype(F32)

    sent_ref[...] = total[...].astype(BF16)


def finish(got_ref, down_ref, up_ref):
    rank = down_ref.shape[1]
    total = got_ref[0].astype(F32)
    for p in range(1, got_ref.shape[0]):
        total = total + got_ref[p].astype(F32)
    down_ref[0] = total[:rank]
    up_ref[0] = unpack(total[rank:], False)[:, :rank].T


def local(
    columns,
    chips,
    activations,
    cotangent,
    key_weight,
    adapter_down,
    adapter_up,
    sequence_tenant,
    slot_holder_tenant,
):
    seqs = sequence_tenant.shape[0]
    rows = activations.shape[0] // seqs
    width = activations.shape[1]
    keys = cotangent.shape[1]
    rank = adapter_down.shape[1]
    slots = slot_holder_tenant.shape[0]
    tall = rank + rank * keys // width
    scale = ADAPTER_SCALE / math.sqrt(seqs * rows)
    struct = jax.ShapeDtypeStruct

    dy = lax.all_gather(cotangent.T, ("y", "c"), axis=0, tiled=True)

    anywhere = pl.BlockSpec(memory_space=pl.ANY)
    near_x = pl.pallas_call(
        bring,
        out_shape=struct(activations.shape, BF16),
        in_specs=[anywhere],
        out_specs=anywhere,
        scratch_shapes=[pltpu.SemaphoreType.DMA],
        compiler_params=PART,
        name="bring_x",
    )(activations)

    tenants = [sequence_tenant] + [
        lax.ppermute(sequence_tenant, "x", [(x, (x + d) % columns) for x in range(columns)])
        for d in range(1, columns)
    ]
    sent = pl.pallas_call(
        prepare,
        out_shape=struct((slots // columns, tall, width), BF16),
        in_specs=[VMEM, VMEM],
        out_specs=VMEM,
        compiler_params=WHOLE,
        name="prepare",
    )(adapter_down, adapter_up)
    panels = lax.all_to_all(sent, "z", 0, 0, tiled=True)
    sent, slot_of, place_of = pl.pallas_call(
        functools.partial(select, columns),
        out_shape=(
            struct((columns, seqs, tall, width), BF16),
            struct((seqs + 1,), jnp.int32),
            struct((columns * seqs,), jnp.int32),
        ),
        in_specs=[VMEM] + [SMEM] * (1 + columns) + [anywhere],
        out_specs=(VMEM, SMEM, SMEM),
        scratch_shapes=[pltpu.SMEM((slots,), jnp.int32)],
        compiler_params=PART,
        name="select",
    )(panels, slot_holder_tenant, *tenants, near_x)
    panels = lax.all_to_all(sent, "x", 0, 0, tiled=True)
    panels, dy = lax.optimization_barrier((panels, dy))
    dy_halves = dy.reshape(chips, 2, keys, dy.shape[1])

    pairs = seqs // 2
    low_u, ups = pl.pallas_call(
        low,
        grid_spec=pltpu.PrefetchScalarGridSpec(
            num_scalar_prefetch=1,
            grid=(pairs,),
            in_specs=[
                pl.BlockSpec(
                    (1, 1, tall, width),
                    lambda p, slot: (slot[2 * p] % columns, 2 * p, 0, 0),
                ),
                pl.BlockSpec(
                    (1, 1, tall, width),
                    lambda p, slot: (slot[2 * p + 1] % columns, 2 * p + 1, 0, 0),
                ),
                pl.BlockSpec((2 * rows, width), lambda p, slot: (p, 0)),
            ],
            out_specs=(
                pl.BlockSpec((1, rows, 2 * rank), lambda p, slot: (p, 0, 0)),
                pl.BlockSpec((1, keys, 2 * rank), lambda p, slot: (p, 0, 0)),
            ),
        ),
        out_shape=(
            struct((pairs, rows, 2 * rank), BF16),
            struct((pairs, keys, 2 * rank), BF16),
        ),
        compiler_params=STEPS,
        name="low",
    )(slot_of, panels, panels, near_x)
    other_low = lax.ppermute(low_u, "c", SWAP)
    down = pl.pallas_call(
        keep,
        out_shape=struct((seqs, rank, width), BF16),
        in_specs=[SMEM, VMEM, anywhere],
        out_specs=VMEM,
        compiler_params=PART,
        name="keep",
    )(slot_of, panels, low_u)
    dy_pair = pl.BlockSpec(
        (chips, 1, keys, 2 * rows), lambda p, slot: (0, slot[seqs], 0, p)
    )
    mixed = pl.BlockSpec((chips, 1, 2 * keys, 2 * rank), lambda p, slot: (0, p, 0, 0))
    sent = pl.pallas_call(
        project,
        grid_spec=pltpu.PrefetchScalarGridSpec(
            num_scalar_prefetch=1,
            grid=(pairs,),
            in_specs=[
                pl.BlockSpec((1, rows, 2 * rank), lambda p, slot: (p, 0, 0)),
                pl.BlockSpec((1, rows, 2 * rank), lambda p, slot: (p, 0, 0)),
                pl.BlockSpec((1, keys, 2 * rank), lambda p, slot: (p, 0, 0)),
                dy_pair,
            ],
            out_specs=mixed,
        ),
        out_shape=struct((chips, pairs, 2 * keys, 2 * rank), BF16),
        compiler_params=STEPS,
        name="project",
    )(slot_of, low_u, other_low, ups, dy_halves)
    got = lax.all_to_all(sent, "y", 0, 0, tiled=True)

    low_g = pl.pallas_call(
        lower,
        grid_spec=pltpu.PrefetchScalarGridSpec(
            num_scalar_prefetch=1,
            grid=(pairs,),
            in_specs=[mixed, dy_pair],
            out_specs=pl.BlockSpec((2, rank, rows), lambda p, slot: (p, 0, 0)),
        ),
        out_shape=struct((seqs, rank, rows), BF16),
        compiler_params=STEPS,
        name="lower",
    )(slot_of, got, dy_halves)
    other_low = lax.ppermute(low_g, "c", SWAP)
    part_b = pl.pallas_call(
        functools.partial(tally, scale),
        in_specs=[VMEM],
        out_specs=VMEM,
        out_shape=struct((seqs, tall - rank, width), F32),
        compiler_params=PART,
        name="tally",
    )(got)
    one = pl.BlockSpec((1, rank, rows), lambda s: (s, 0, 0))
    low_g, sent = pl.pallas_call(
        functools.partial(combine, scale),
        grid=(seqs,),
        in_specs=[
            one,
            one,
            pl.BlockSpec((1, tall - rank, width), lambda s: (s, 0, 0)),
            pl.BlockSpec((rows, width), lambda s: (s, 0)),
        ],
        out_specs=(one, pl.BlockSpec((columns, 1, tall, width), lambda s: (0, s, 0, 0))),
        out_shape=(
            struct((seqs, rank, rows), BF16),
            struct((columns, seqs, tall, width), BF16),
        ),
        compiler_params=STEPS,
        name="combine",
    )(low_g, other_low, part_b, near_x)
    input_gradient = pl.pallas_call(
        backward,
        grid=(seqs,),
        in_specs=[
            one,
            pl.BlockSpec((dy.shape[0], rows), lambda s: (0, s)),
            pl.BlockSpec(key_weight.shape, lambda s: (0, 0)),
            pl.BlockSpec((1, rank, width), lambda s: (s, 0, 0)),
        ],
        out_specs=pl.BlockSpec((rows, width), lambda s: (s, 0)),
        out_shape=struct(activations.shape, BF16),
        compiler_params=ALL,
        cost_estimate=pl.CostEstimate(
            flops=2 * activations.shape[0] * width * (key_weight.shape[1] + rank),
            bytes_accessed=2 * (activations.shape[0] + width) * (key_weight.shape[1] + width),
            transcendentals=0,
        ),
        name="backward",
    )(low_g, dy, key_weight, down)
    got = lax.all_to_all(sent, "x", 0, 0, tiled=True)

    sent = pl.pallas_call(
        sort,
        out_shape=struct((slots // columns, tall, width), BF16),
        in_specs=[SMEM, VMEM],
        out_specs=VMEM,
        scratch_shapes=[pltpu.VMEM((slots // columns, tall, width), F32)],
        compiler_params=PART,
        name="sort",
    )(place_of, got)
    got = lax.all_to_all(sent, "z", 0, 0, tiled=True)

    grad_a, grad_b = pl.pallas_call(
        finish,
        out_shape=(struct((1, rank, width), F32), struct((1, rank, keys), F32)),
        in_specs=[VMEM],
        out_specs=(VMEM, VMEM),
        compiler_params=PART,
        name="finish",
    )(got)
    return (input_gradient, grad_a, grad_b)


def solution(mesh):
    columns = min(COLUMNS, mesh.shape["dp"] // 2)
    chips = mesh.shape["mp"] // 2
    grid = Mesh(mesh.devices.reshape(-1, columns, chips, 2), ("z", "x", "y", "c"))
    dp, mp = ("z", "x"), ("y", "c")
    in_specs = (
        P(dp, mp),
        P(dp, mp),
        P(mp, None),
        P(dp, None, mp),
        P(dp, None, mp),
        P(dp),
        P(),
    )
    out_specs = (P(dp, mp), P(dp, None, mp), P(dp, None, mp))
    body = functools.partial(local, columns, chips)
    return jax.shard_map(body, mesh=grid, in_specs=in_specs, out_specs=out_specs, check_vma=False)
```
